32 devices in a mesh: dom: 8 (over z, y), tile: 4 (over x, core).
Axes of the slice: x: 2, y: 2, z: 4, core: 2. Of those that a mesh axis runs over, the one named last changes fastest.
Arguments:
- features: bfloat16 [16384, 256], P(('dom', 'tile')), may hold values from -6 to 6
- grad_out: bfloat16 [16384, 256], P(('dom', 'tile')), may hold values from -6 to 6
- self_weight: bfloat16 [256, 256], replicated, may hold values from -0.375 to 0.375
- neigh_weight: bfloat16 [256, 256], replicated, may hold values from -0.375 to 0.375
- edge_tiles: bfloat16 [2304, 128, 128], P(('dom', 'tile')), may hold values from 0 to 1.5, as said below
- tile_dst: int32 [2304], P(('dom', 'tile')), may hold values from 0 to 15
- tile_src: int32 [2304], P(('dom', 'tile')), may hold values from 0 to 25
- halo_send: int32 [8, 1024], P('dom'), may hold values from 0 to 2047
- hub_ids: int32 [256], P('dom'), may hold values from 0 to 2047
Outputs:
- activated: bfloat16 [16384, 256], P(('dom', 'tile'))
- grad_features: bfloat16 [16384, 256], P(('dom', 'tile'))
- grad_self_weight: float32 [256, 256], replicated
- grad_neigh_weight: float32 [256, 256], replicated
The draws below stay inside these ranges and needn't reach their ends.
Inputs may be any that keep to these rules, and one draw needn't show every extreme that they name: `edge_tiles`: each entry is zero or an edge weight of 0.3 or more.
All inputs are finite; a program needn't handle non-finite values.
Results may differ from the reference program's by a relative error of at most 0.014.
Values may be sent and summed in bfloat16 or wider, within the bound.
A program may use at most 64 MiB of HBM per device.

```python
import math
import jax
import jax.numpy as jnp
import numpy as np
from jax import lax

F = 256
H = 256
TB = 128
V_DEV = 2048
TILE_DEV = 72
HALO_ROWS = 1024
HUBS = 256
NODES = 16384
SRC = 3328
TILES = 2304
N_DOM = 8
N_TILE = 4


def draw_edge_tiles(key, part):
    key_rate = jax.random.fold_in(key, 11)
    key_keep = jax.random.fold_in(key, 12)
    key_value = jax.random.fold_in(key, 13)
    rate = jax.random.uniform(key_rate, (TILES, TB, 1), jnp.float32, 0.002, 0.03)
    keep = jax.random.uniform(key_keep, (TILES, TB, TB), jnp.float32) < rate
    values = jnp.exp(jax.random.uniform(key_value, (TILES, TB, TB), jnp.float32, math.log(0.3), math.log(1.5)))
    return jnp.where(keep, values, 0.0).astype(jnp.bfloat16)


def set_ends(drawn, own_key, least, high):
    longest = drawn.shape.index(max(drawn.shape))
    spots = []
    for shift in (0, 1):
        where = [jax.random.randint(jax.random.fold_in(own_key, axis), (), 0, length) for axis, length in enumerate(drawn.shape)]
        where[longest] = (where[longest] + shift) % drawn.shape[longest]
        spots.append(tuple(where))
    return drawn.at[spots[0]].set(least).at[spots[1]].set(high)


def level_of(key, extent, pieces, smallest, top_value):
    def one(position, blocks):
        steps = jax.random.uniform(jax.random.fold_in(jax.random.fold_in(key, 6), position), (blocks,), jnp.float32, smallest / len(pieces), top_value / len(pieces))
        return jnp.repeat(jnp.exp(steps), extent[position] // blocks).reshape((-1,) + (1,) * (len(extent) - position - 1))

    factor_of = one(*pieces[0])
    for cut in pieces[1:]:
        factor_of = factor_of * one(*cut)
    return factor_of


def rank_bounds(number_of, lean):
    weights = [(1 << 20) // math.isqrt(rank ** lean) + 1 for rank in range(1, number_of + 1)]
    scale = 1 + sum(weights) // (1 << 30)
    return np.cumsum(np.array([max(1, weight // scale) for weight in weights]))


def ranked_ids(own_key, extent, amount, lean):
    table = rank_bounds(amount, lean)
    pick = jax.random.randint(jax.random.fold_in(own_key, 1), extent, 0, int(table[amount - 1]))
    standing = jnp.searchsorted(jnp.asarray(table, jnp.int32), pick, side="right")
    return jax.random.permutation(jax.random.fold_in(own_key, 2), amount)[standing].astype(jnp.int32)


def centred(stream_key, extent, width, reach, pieces=(), kind=jnp.bfloat16):
    array = width * jax.random.normal(stream_key, extent, jnp.float32)
    if pieces:
        array = array * level_of(stream_key, extent, pieces, -0.22, 0.18)
    return jnp.clip(array, -reach, reach).astype(kind)


def setup_inputs(seed: int = 0) -> dict:
    key_of = jax.random.split(jax.random.key(seed), 10)
    features = centred(key_of[0], (NODES, F), 1.0, 6.0, ((0, 32),))
    grad_out = centred(key_of[1], (NODES, H), 1.0, 6.0, ((0, 32),))
    self_weight = centred(key_of[2], (F, H), F ** -0.5, 0.375)
    neigh_weight = centred(key_of[3], (F, H), F ** -0.5, 0.375)
    edge_tiles = draw_edge_tiles(jax.random.fold_in(key_of[9], 71), 0)
    tile_dst = set_ends(ranked_ids(key_of[5], (TILES,), V_DEV // TB, 2), jax.random.fold_in(key_of[5], 3), 0, (V_DEV // TB) - 1).astype(jnp.int32)
    tile_src = set_ends(jax.random.randint(key_of[6], (TILES,), 0, SRC // TB), jax.random.fold_in(key_of[6], 1), 0, (SRC // TB) - 1).astype(jnp.int32)
    halo_send = set_ends(jax.random.randint(key_of[7], (N_DOM, HALO_ROWS), 0, V_DEV), jax.random.fold_in(key_of[7], 1), 0, V_DEV - 1).astype(jnp.int32)
    hub_ids = set_ends(jax.random.randint(key_of[8], (HUBS,), 0, V_DEV), jax.random.fold_in(key_of[8], 1), 0, V_DEV - 1).astype(jnp.int32)
    return dict(features=features, grad_out=grad_out, self_weight=self_weight, neigh_weight=neigh_weight, edge_tiles=edge_tiles, tile_dst=tile_dst, tile_src=tile_src, halo_send=halo_send, hub_ids=hub_ids)


def block_onehot(indices, number):
    return (indices[None, :] == jnp.arange(number, dtype=jnp.int32)[:, None]).astype(jnp.float32)


def settle(values):
    return lax.optimization_barrier(values.astype(jnp.bfloat16)).astype(jnp.float32)


def reference(features, grad_out, self_weight, neigh_weight, edge_tiles, tile_dst, tile_src, halo_send, hub_ids):
    per_peer = HALO_ROWS // N_DOM
    hub_own = HUBS // N_DOM
    src_rows = V_DEV + HALO_ROWS + HUBS
    src_blocks = src_rows // TB
    dst_blocks = V_DEV // TB
    by_domain = features.reshape(N_DOM, V_DEV, F)
    domain_ids = jnp.arange(N_DOM, dtype=jnp.int32)[:, None]
    hub_table = by_domain[domain_ids, hub_ids.reshape(N_DOM, hub_own)].reshape(HUBS, F)
    tiles_dom = edge_tiles.reshape(N_DOM, N_TILE, TILE_DEV, TB, TB)
    dst_dom = tile_dst.reshape(N_DOM, N_TILE, TILE_DEV)
    src_dom = tile_src.reshape(N_DOM, N_TILE, TILE_DEV)

    def forward_part(part):
        local = by_domain[part]
        chosen = lax.dynamic_slice_in_dim(halo_send, part * per_peer, per_peer, 1)
        halo = by_domain[domain_ids, chosen].reshape(HALO_ROWS, F)
        source = jnp.concatenate([local, halo, hub_table], axis=0).reshape(src_blocks, TB, F)
        summed = jnp.zeros((V_DEV, F), jnp.float32)
        degree = jnp.zeros((V_DEV,), jnp.float32)
        for group in range(N_TILE):
            tiles = tiles_dom[part, group].astype(jnp.float32)
            picked = source[src_dom[part, group]].astype(jnp.float32)
            products = jnp.einsum("tij,tjf->tif", tiles, picked, precision=lax.Precision.HIGHEST)
            into_dest = block_onehot(dst_dom[part, group], dst_blocks)
            partial_value = jnp.einsum("dt,tif->dif", into_dest, products, precision=lax.Precision.HIGHEST).reshape(V_DEV, F)
            row_weight = jnp.sum(tiles, axis=2)
            part_deg = jnp.dot(into_dest, row_weight, precision=lax.Precision.HIGHEST).reshape(V_DEV)
            summed = summed + settle(partial_value)
            degree = degree + settle(part_deg)
        return summed, degree

    summed_all, degree_all = lax.map(forward_part, jnp.arange(N_DOM, dtype=jnp.int32))
    summed_all = summed_all.reshape(NODES, F)
    divisor = jnp.maximum(degree_all.reshape(NODES), 1.0)
    mean_rows = (summed_all / divisor[:, None]).astype(jnp.bfloat16)
    hidden = jnp.dot(features, self_weight, preferred_element_type=jnp.float32) + jnp.dot(mean_rows, neigh_weight, preferred_element_type=jnp.float32)
    activated = jax.nn.silu(hidden).astype(jnp.bfloat16)
    sigmoid_h = jax.nn.sigmoid(hidden)
    grad_hidden = (grad_out.astype(jnp.float32) * sigmoid_h * (1.0 + hidden * (1.0 - sigmoid_h))).astype(jnp.bfloat16)
    inv_root = 1.0 / (NODES ** 0.5)
    grad_self_weight = jnp.einsum("nf,nh->fh", features.astype(jnp.float32), grad_hidden.astype(jnp.float32), precision=lax.Precision.HIGHEST) * inv_root
    grad_neigh_weight = jnp.einsum("nf,nh->fh", mean_rows.astype(jnp.float32), grad_hidden.astype(jnp.float32), precision=lax.Precision.HIGHEST) * inv_root
    grad_mean = jnp.dot(grad_hidden, neigh_weight.T, preferred_element_type=jnp.float32) / divisor[:, None]
    grad_mean_b = grad_mean.astype(jnp.bfloat16).reshape(N_DOM, dst_blocks, TB, F)

    def backward_part(part):
        grad_local = jnp.zeros((V_DEV, F), jnp.float32)
        grad_remote = jnp.zeros((HALO_ROWS + HUBS, F), jnp.float32)
        for group in range(N_TILE):
            tiles = tiles_dom[part, group].astype(jnp.float32)
            dst_pick = grad_mean_b[part][dst_dom[part, group]].astype(jnp.float32)
            back_prod = jnp.einsum("tij,tif->tjf", tiles, dst_pick, precision=lax.Precision.HIGHEST)
            into_source = block_onehot(src_dom[part, group], src_blocks)
            partial_src = jnp.einsum("st,tjf->sjf", into_source, back_prod, precision=lax.Precision.HIGHEST).reshape(src_rows, F)
            grad_local = grad_local + settle(partial_src[:V_DEV])
            grad_remote = grad_remote + partial_src[V_DEV:]
        return grad_local, grad_remote

    local_all, remote_all = lax.map(backward_part, jnp.arange(N_DOM, dtype=jnp.int32))
    halo_parts = remote_all[:, :HALO_ROWS].reshape(N_DOM, N_DOM, per_peer, F)
    halo_parts = jnp.transpose(halo_parts, (1, 0, 2, 3)).reshape(N_DOM, HALO_ROWS, F)
    hub_sum = jnp.sum(remote_all[:, HALO_ROWS:], axis=0).reshape(N_DOM, hub_own, F)

    def spread_one(halo_rows, halo_index, hub_rows, hub_index):
        spread = jnp.zeros((V_DEV, F), jnp.float32).at[halo_index].add(halo_rows)
        return spread.at[hub_index].add(hub_rows)

    returned = jax.vmap(spread_one)(halo_parts, halo_send, hub_sum, hub_ids.reshape(N_DOM, hub_own))
    grad_features = jnp.dot(grad_hidden, self_weight.T, preferred_element_type=jnp.float32) + local_all.reshape(NODES, F) + returned.reshape(NODES, F)
    return activated, grad_features.astype(jnp.bfloat16), grad_self_weight, grad_neigh_weight
```

```python
import functools

import jax
import jax.numpy as jnp
from jax import lax
from jax.experimental import pallas as pl
from jax.experimental.pallas import tpu as pltpu
from jax.sharding import PartitionSpec as P

BF = jnp.bfloat16
F32 = jnp.float32
MESH = pl.DeviceIdType.MESH
VMEM = pl.BlockSpec(memory_space=pltpu.VMEM)
SMEM = pl.BlockSpec(memory_space=pltpu.SMEM)
ANY = pl.BlockSpec(memory_space=pl.ANY)
LIMIT = 40 * 1024 * 1024
NT = (((1,), (1,)), ((), ()))
TN = (((0,), (0,)), ((), ()))


def places(domains):
    me = lax.axis_index("dom")
    t = lax.axis_index("tile")
    core = t + 1 - 2 * lax.rem(t, 2)
    across = lax.rem(t + 2, 4)
    diagonal = lax.rem(core + 2, 4)

    def slots(who):
        first = lax.rem(who + 4 * domains - me, 4)
        return lambda i: first + 4 * i

    return me, t, core, across, diagonal, slots


def remote(src, dst, send, recv, **device):
    return pltpu.make_async_remote_copy(
        src_ref=src,
        dst_ref=dst,
        send_sem=send,
        recv_sem=recv,
        device_id=device,
        device_id_type=MESH,
    )


def greet(me, peers, others, count):
    barrier = pltpu.get_barrier_semaphore()
    for peer in peers:
        pl.semaphore_signal(barrier, inc=1, device_id={"tile": peer}, device_id_type=MESH)
    for i in range(count):
        there = others(i)

        @pl.when(there != me)
        def _():
            pl.semaphore_signal(barrier, inc=1, device_id={"dom": there}, device_id_type=MESH)

    own = jnp.where(lax.rem(others(0) + 4 * count - me, 4) == 0, 1, 0) if count else 0
    pl.semaphore_wait(barrier, len(peers) + count - own)


def each(count, body):
    if count <= 4:
        for i in range(count):
            body(i)
    else:

        def step(i, carry):
            body(i)
            return carry

        lax.fori_loop(0, count, step, 0)


def dom_send(count, me, own_slots, pairs):
    def body(i):
        there = own_slots(i)
        for staged, landing, send, recv in pairs:

            @pl.when(there != me)
            def _():
                remote(staged.at[i], landing.at[me], send.at[i], recv.at[me], dom=there).start()

            @pl.when(there == me)
            def _():
                landing[me] = staged[i]

    each(count, body)


def dom_gather(count, me, t, core, across, diagonal, slots, pairs, forward):
    mine, theirs = slots(t), slots(across)

    def first(i):
        there = mine(i)
        for (staged, landing, send, recv), (fcore, facross) in zip(pairs, forward):

            @pl.when(there != me)
            def _():
                copy = remote(staged.at[i], landing.at[there], send.at[i], recv.at[there], dom=there)
                copy.wait_send()
                copy.wait_recv()

            spot = landing.at[there]
            remote(spot, spot, facross.at[there], recv.at[there], tile=across).start()
            remote(spot, spot, fcore.at[there], recv.at[there], tile=core).start()

    each(count, first)

    def second(i):
        there = theirs(i)
        for (staged, landing, send, recv), (fcore, facross) in zip(pairs, forward):
            spot = landing.at[there]
            remote(spot, spot, facross.at[there], recv.at[there], tile=across).wait_recv()
            remote(spot, spot, fcore.at[there], recv.at[there], tile=core).start()

    each(count, second)

    def third(i):
        for (staged, landing, send, recv), (fcore, facross) in zip(pairs, forward):
            for who in (core, diagonal):
                there = slots(who)(i)
                spot = landing.at[there]
                remote(spot, spot, fcore.at[there], recv.at[there], tile=core).wait_recv()
            for there, sem, peer in (
                (mine(i), facross, across),
                (mine(i), fcore, core),
                (theirs(i), fcore, core),
            ):
                spot = landing.at[there]
                remote(spot, spot, sem.at[there], recv.at[there], tile=peer).wait_send()

    each(count, third)


def tile_gather_start(src, out, t, core, across, send, recv):
    remote(src, out.at[t], send.at[0], recv.at[t], tile=across).start()
    remote(src, out.at[t], send.at[1], recv.at[t], tile=core).start()


def tile_gather_middle(out, core, across, send, recv):
    spot = out.at[across]
    remote(spot, spot, send.at[0], recv.at[across], tile=across).wait_recv()
    remote(spot, spot, send.at[2], recv.at[across], tile=core).start()


def tile_gather_end(src, out, core, across, diagonal, send, recv):
    for who in (core, diagonal):
        remote(out.at[who], out.at[who], send.at[1], recv.at[who], tile=core).wait_recv()
    remote(src, out.at[core], send.at[0], recv.at[core], tile=across).wait_send()
    remote(src, out.at[core], send.at[1], recv.at[core], tile=core).wait_send()
    remote(out.at[across], out.at[across], send.at[2], recv.at[core], tile=core).wait_send()


def collect_kernel(
    domains,
    feat,
    halo_ids,
    hub_ids,
    local,
    halo,
    hub,
    staged_halo,
    staged_hub,
    tile_send,
    tile_recv,
    halo_send,
    hub_send,
    halo_recv,
    hub_recv,
    halo_core,
    halo_across,
    hub_core,
    hub_across,
):
    count = domains // 4
    me, t, core, across, diagonal, slots = places(domains)
    mine = slots(t)
    quarter = feat.shape[0]
    greet(me, (core, across, diagonal), mine, count)
    tile_gather_start(feat, local, t, core, across, tile_send, tile_recv)
    local[t] = feat[...]
    tile_gather_middle(local, core, across, tile_send, tile_recv)
    tile_gather_end(feat, local, core, across, diagonal, tile_send, tile_recv)

    def rows(ids):
        total = None
        for part in range(4):
            spot = lax.broadcasted_iota(jnp.int32, (quarter, ids.shape[1]), 0) + part * quarter
            chosen = (spot == ids).astype(F32).astype(BF)
            term = lax.dot_general(chosen, local[part], TN, preferred_element_type=F32)
            total = term if total is None else total + term
        return total.astype(BF)

    own_hubs = rows(hub_ids[...])

    def body(i):
        staged_hub[i] = own_hubs
        staged_halo[i] = rows(halo_ids[mine(i)])

    each(count, body)
    pairs = ((staged_halo, halo, halo_send, halo_recv), (staged_hub, hub, hub_send, hub_recv))
    forward = ((halo_core, halo_across), (hub_core, hub_across))
    dom_send(count, me, mine, pairs)
    dom_gather(count, me, t, core, across, diagonal, slots, pairs, forward)


def forward_kernel(tiles, dst, src, local, halo, hub, out, deg, source, acc, sems):
    nl, nh = local.shape[0], halo.shape[0]
    copies = [
        pltpu.make_async_copy(local, source.at[pl.ds(0, nl)], sems.at[0]),
        pltpu.make_async_copy(halo, source.at[pl.ds(nl, nh)], sems.at[1]),
        pltpu.make_async_copy(hub, source.at[pl.ds(nl + nh, hub.shape[0])], sems.at[2]),
    ]
    for copy in copies:
        copy.start()
    acc[...] = jnp.zeros_like(acc)
    deg[...] = jnp.zeros_like(deg)
    ones = jnp.ones((8, tiles.shape[2]), BF)
    for copy in copies:
        copy.wait()
    step = 4

    def body(k, carry):
        found = []
        for i in range(step):
            j = k * step + i
            e = tiles[j]
            found.append(
                (
                    dst[j],
                    jnp.dot(e, source[src[j]], preferred_element_type=F32),
                    lax.dot_general(ones, e, NT, preferred_element_type=F32),
                )
            )
        for d, product, weight in found:
            acc[d] += product
            deg[d] += weight
        return carry

    lax.fori_loop(0, tiles.shape[0] // step, body, 0)
    out[...] = acc[...].astype(BF)


def backward_kernel(tiles, dst, src, grad, local, halo, hub, acc):
    nl, nh = local.shape[0], halo.shape[0]
    acc[...] = jnp.zeros_like(acc)
    step = 4

    def body(k, carry):
        found = []
        for i in range(step):
            j = k * step + i
            found.append(
                (
                    src[j],
                    lax.dot_general(tiles[j], grad[dst[j]], TN, preferred_element_type=F32),
                )
            )
        for s, product in found:
            acc[s] += product
        return carry

    lax.fori_loop(0, tiles.shape[0] // step, body, 0)
    local[...] = acc[pl.ds(0, nl)].astype(BF)
    halo[...] = acc[pl.ds(nl, nh)].astype(BF)
    hub[...] = acc[pl.ds(nl + nh, hub.shape[0])].astype(BF)


def pair_send(partial, landing, send, recv, core, diagonal):
    remote(partial.at[diagonal], landing.at[1], send.at[1], recv.at[1], tile=core).start()
    remote(partial.at[core], landing.at[0], send.at[0], recv.at[0], tile=core).start()


def dense_kernel(
    domains,
    partial,
    deg,
    feat,
    grad_out,
    self_weight,
    neigh_weight,
    activated,
    grad_hidden,
    grad_all,
    self_term,
    neigh_term,
    landing,
    other,
    passing,
    deg_in,
    mine_b,
    pair_sems,
    pair_recv,
    cross_sem,
    cross_recv,
    deg_send,
    deg_recv,
    tile_send,
    tile_recv,
):
    me, t, core, across, diagonal, slots = places(domains)
    greet(me, (core, across, diagonal), None, 0)
    pair_send(partial, landing, pair_sems, pair_recv, core, diagonal)
    peers = (core, across, diagonal)
    for i, peer in enumerate(peers):
        remote(deg.at[peer], deg_in.at[i], deg_send.at[i], deg_recv.at[i], tile=peer).start()
    first = remote(partial.at[across], landing.at[1], pair_sems.at[1], pair_recv.at[1], tile=core)
    first.wait_recv()
    passing[...] = (partial[across].astype(F32) + landing[1].astype(F32)).astype(BF)
    cross = remote(passing, other, cross_sem, cross_recv, tile=across)
    cross.start()
    hidden = jnp.dot(feat[...], self_weight[...], preferred_element_type=F32)
    second = remote(partial.at[core], landing.at[0], pair_sems.at[0], pair_recv.at[0], tile=core)
    second.wait_recv()
    degree = deg[t]
    for i, peer in enumerate(peers):
        copy = remote(deg.at[peer], deg_in.at[i], deg_send.at[i], deg_recv.at[i], tile=peer)
        copy.wait_recv()
        degree = degree + deg_in[i]
    blocks, _, size = degree.shape
    columns = feat.shape[1]
    scale = 1.0 / jnp.maximum(degree, 1.0)
    pieces = []
    for b in range(blocks):
        turned = jnp.broadcast_to(scale[b, 0:1, :], (size, size)).T
        pieces.append(jnp.concatenate([turned] * (columns // size), axis=1))
    inverse = jnp.concatenate(pieces, axis=0)
    cross.wait_recv()
    summed = partial[t].astype(F32) + landing[0].astype(F32) + other[...].astype(F32)
    mean_rows = (summed * inverse).astype(BF)
    hidden = hidden + jnp.dot(mean_rows, neigh_weight[...], preferred_element_type=F32)
    sig = jax.nn.sigmoid(hidden)
    grads = (grad_out[...].astype(F32) * sig * (1.0 + hidden * (1.0 - sig))).astype(BF)
    back = lax.dot_general(grads, neigh_weight[...], NT, preferred_element_type=F32)
    mine_b[...] = (back * inverse).astype(BF)
    tile_gather_start(mine_b, grad_all, t, core, across, tile_send, tile_recv)
    grad_all[t] = mine_b[...]
    activated[...] = (hidden * sig).astype(BF)
    grad_hidden[...] = grads
    self_term[...] = lax.dot_general(feat[...], grads, TN, preferred_element_type=F32)
    tile_gather_middle(grad_all, core, across, tile_send, tile_recv)
    neigh_term[...] = lax.dot_general(mean_rows, grads, TN, preferred_element_type=F32)
    tile_gather_end(mine_b, grad_all, core, across, diagonal, tile_send, tile_recv)
    first.wait_send()
    second.wait_send()
    cross.wait_send()
    for i, peer in enumerate(peers):
        remote(deg.at[peer], deg_in.at[i], deg_send.at[i], deg_recv.at[i], tile=peer).wait_send()


def return_kernel(
    domains,
    local,
    halo,
    hub,
    halo_ids,
    hub_ids,
    grad_hidden,
    self_weight,
    out,
    landing,
    other,
    passing,
    halo_in,
    hub_in,
    halo_pass,
    hub_pass,
    halo_other,
    hub_other,
    halo_total,
    hub_total,
    halo_back,
    hub_back,
    acc,
    pair_sems,
    pair_recv,
    cross_sem,
    cross_recv,
    halo_send,
    hub_send,
    halo_recv,
    hub_recv,
    halo_csend,
    hub_csend,
    halo_crecv,
    hub_crecv,
    halo_dsend,
    hub_dsend,
    halo_drecv,
    hub_drecv,
    halo_core,
    halo_across,
    hub_core,
    hub_across,
):
    count = domains // 4
    me, t, core, across, diagonal, slots = places(domains)
    mine, theirs = slots(t), slots(across)
    quarter = out.shape[0]
    greet(me, (core, across, diagonal), mine, count)
    both = (
        (halo, halo_in, halo_send, halo_recv, halo_pass, halo_other, halo_csend, halo_crecv, halo_total),
        (hub, hub_in, hub_send, hub_recv, hub_pass, hub_other, hub_csend, hub_crecv, hub_total),
    )

    def start_for(who):
        spots = slots(who)

        def body(i):
            s = spots(i)
            for part, landed, send, recv, *_ in both:
                remote(part.at[s], landed.at[s], send.at[s], recv.at[s], tile=core).start()

        each(count, body)

    start_for(diagonal)
    start_for(core)
    pair_send(local, landing, pair_sems, pair_recv, core, diagonal)

    def pass_on(i):
        s = theirs(i)
        for part, landed, send, recv, passed, crossed, csend, crecv, total in both:
            remote(part.at[s], landed.at[s], send.at[s], recv.at[s], tile=core).wait_recv()
            passed[i] = (part[s].astype(F32) + landed[s].astype(F32)).astype(BF)
            remote(passed.at[i], crossed.at[i], csend.at[i], crecv.at[i], tile=across).start()

    each(count, pass_on)
    first = remote(local.at[across], landing.at[1], pair_sems.at[1], pair_recv.at[1], tile=core)
    first.wait_recv()
    passing[...] = (local[across].astype(F32) + landing[1].astype(F32)).astype(BF)
    cross = remote(passing, other, cross_sem, cross_recv, tile=across)

    def own(i):
        s = mine(i)
        for part, landed, send, recv, passed, crossed, csend, crecv, total in both:
            remote(part.at[s], landed.at[s], send.at[s], recv.at[s], tile=core).wait_recv()
            remote(passed.at[i], crossed.at[i], csend.at[i], crecv.at[i], tile=across).wait_recv()
            total[i] = (part[s].astype(F32) + landed[s].astype(F32) + crossed[i].astype(F32)).astype(BF)

    each(count, own)
    pairs = (
        (halo_total, halo_back, halo_dsend, halo_drecv),
        (hub_total, hub_back, hub_dsend, hub_drecv),
    )
    forward = ((halo_core, halo_across), (hub_core, hub_across))
    dom_send(count, me, mine, pairs)
    cross.start()
    acc[...] = lax.dot_general(grad_hidden[...], self_weight[...], NT, preferred_element_type=F32)
    second = remote(local.at[core], landing.at[0], pair_sems.at[0], pair_recv.at[0], tile=core)
    second.wait_recv()
    acc[...] += local[t].astype(F32) + landing[0].astype(F32)
    dom_gather(count, me, t, core, across, diagonal, slots, pairs, forward)

    def pick(ids):
        spot = lax.broadcasted_iota(jnp.int32, (quarter, ids.shape[1]), 0) + t * quarter
        return (spot == ids).astype(F32).astype(BF)

    hub_pick = pick(hub_ids[...])

    def spread(p, carry):
        acc[...] += jnp.dot(pick(halo_ids[p]), halo_back[p], preferred_element_type=F32) + jnp.dot(
            hub_pick, hub_back[p], preferred_element_type=F32
        )
        return carry

    lax.fori_loop(0, domains, spread, 0)
    cross.wait_recv()
    out[...] = (acc[...] + other[...].astype(F32)).astype(BF)
    first.wait_send()
    second.wait_send()
    cross.wait_send()

    def finish(i):
        for part, landed, send, recv, passed, crossed, csend, crecv, total in both:
            for who in (core, diagonal):
                s = slots(who)(i)
                remote(part.at[s], landed.at[s], send.at[s], recv.at[s], tile=core).wait_send()
            remote(passed.at[i], crossed.at[i], csend.at[i], crecv.at[i], tile=across).wait_send()

    each(count, finish)


def on_device(
    features,
    grad_out,
    self_weight,
    neigh_weight,
    edge_tiles,
    tile_dst,
    tile_src,
    halo_send,
    hub_ids,
):
    domains = lax.axis_size("dom")
    groups = lax.axis_size("tile")
    quarter, columns = features.shape
    size = edge_tiles.shape[1]
    vertices = quarter * groups
    halo_total = halo_send.shape[1]
    per_peer = halo_total // domains
    hub_own = hub_ids.shape[0]
    hubs = hub_own * domains
    count = domains // groups
    outs = grad_out.shape[1]
    nl, nh, nb = vertices // size, halo_total // size, hubs // size
    halo_ids = halo_send.reshape(domains, 1, per_peer)
    hub_row = hub_ids.reshape(1, hub_own)
    sem = lambda n: pltpu.SemaphoreType.DMA((n,))
    shape = jax.ShapeDtypeStruct

    def params(number):
        return pltpu.CompilerParams(
            collective_id=number, has_side_effects=True, vmem_limit_bytes=LIMIT
        )

    local, halo, hub = pl.pallas_call(
        functools.partial(collect_kernel, domains),
        out_shape=(
            shape((groups, quarter, columns), BF),
            shape((domains, per_peer, columns), BF),
            shape((domains, hub_own, columns), BF),
        ),
        in_specs=[VMEM] * 3,
        out_specs=(VMEM,) * 3,
        scratch_shapes=[
            pltpu.VMEM((count, per_peer, columns), BF),
            pltpu.VMEM((count, hub_own, columns), BF),
            sem(3),
            sem(4),
            sem(count),
            sem(count),
        ]
        + [sem(domains)] * 6,
        compiler_params=params(0),
        name="collect",
    )(features, halo_ids, hub_row)

    partial, degree = pl.pallas_call(
        forward_kernel,
        out_shape=(shape((nl, size, columns), BF), shape((nl, 8, size), F32)),
        in_specs=[VMEM, SMEM, SMEM, ANY, ANY, ANY],
        out_specs=(VMEM, VMEM),
        scratch_shapes=[
            pltpu.VMEM((nl + nh + nb, size, columns), BF),
            pltpu.VMEM((nl, size, columns), F32),
            sem(3),
        ],
        compiler_params=pltpu.CompilerParams(vmem_limit_bytes=LIMIT),
        name="aggregate",
    )(
        edge_tiles,
        tile_dst,
        tile_src,
        local.reshape(nl, size, columns),
        halo.reshape(nh, size, columns),
        hub.reshape(nb, size, columns),
    )

    block = pltpu.VMEM((quarter, columns), BF)
    activated, grad_hidden, grad_all, self_term, neigh_term = pl.pallas_call(
        functools.partial(dense_kernel, domains),
        out_shape=(
            shape((quarter, outs), BF),
            shape((quarter, outs), BF),
            shape((groups, quarter, columns), BF),
            shape((columns, outs), F32),
            shape((columns, outs), F32),
        ),
        in_specs=[VMEM] * 6,
        out_specs=(VMEM,) * 5,
        scratch_shapes=[
            pltpu.VMEM((2, quarter, columns), BF),
            block,
            block,
            pltpu.VMEM((3, nl // groups, 8, size), F32),
            block,
            sem(2),
            sem(2),
            pltpu.SemaphoreType.DMA,
            pltpu.SemaphoreType.DMA,
            sem(3),
            sem(3),
            sem(3),
            sem(4),
        ],
        compiler_params=params(1),
        name="dense",
    )(
        partial.reshape(groups, quarter, columns),
        degree.reshape(groups, nl // groups, 8, size),
        features,
        grad_out,
        self_weight,
        neigh_weight,
    )

    inv_root = 1.0 / (vertices * domains) ** 0.5
    grad_self, grad_neigh = lax.psum((self_term, neigh_term), ("dom", "tile"))

    back_local, back_halo, back_hub = pl.pallas_call(
        backward_kernel,
        out_shape=(
            shape((nl, size, columns), BF),
            shape((nh, size, columns), BF),
            shape((nb, size, columns), BF),
        ),
        in_specs=[VMEM, SMEM, SMEM, VMEM],
        out_specs=(VMEM,) * 3,
        scratch_shapes=[pltpu.VMEM((nl + nh + nb, size, columns), F32)],
        compiler_params=pltpu.CompilerParams(vmem_limit_bytes=LIMIT),
        name="backward",
    )(edge_tiles, tile_dst, tile_src, grad_all.reshape(nl, size, columns))

    grad_features = pl.pallas_call(
        functools.partial(return_kernel, domains),
        out_shape=shape((quarter, columns), BF),
        in_specs=[VMEM] * 7,
        out_specs=VMEM,
        scratch_shapes=[
            pltpu.VMEM((2, quarter, columns), BF),
            block,
            block,
            pltpu.VMEM((domains, per_peer, columns), BF),
            pltpu.VMEM((domains, hub_own, columns), BF),
            pltpu.VMEM((count, per_peer, columns), BF),
            pltpu.VMEM((count, hub_own, columns), BF),
            pltpu.VMEM((count, per_peer, columns), BF),
            pltpu.VMEM((count, hub_own, columns), BF),
            pltpu.VMEM((count, per_peer, columns), BF),
            pltpu.VMEM((count, hub_own, columns), BF),
            pltpu.VMEM((domains, per_peer, columns), BF),
            pltpu.VMEM((domains, hub_own, columns), BF),
            pltpu.VMEM((quarter, columns), F32),
            sem(2),
            sem(2),
            pltpu.SemaphoreType.DMA,
            pltpu.SemaphoreType.DMA,
        ]
        + [sem(domains)] * 4
        + [sem(count)] * 4
        + [sem(count)] * 2
        + [sem(domains)] * 2
        + [sem(domains)] * 4,
        compiler_params=params(2),
        name="give_back",
    )(
        back_local.reshape(groups, quarter, columns),
        back_halo.reshape(domains, per_peer, columns),
        back_hub.reshape(domains, hub_own, columns),
        halo_ids,
        hub_row,
        grad_hidden,
        self_weight,
    )
    return activated, grad_features, grad_self * inv_root, grad_neigh * inv_root


def solution(mesh):
    return jax.shard_map(
        on_device,
        mesh=mesh,
        in_specs=(
            P(("dom", "tile"), None),
            P(("dom", "tile"), None),
            P(),
            P(),
            P(("dom", "tile"), None, None),
            P(("dom", "tile")),
            P(("dom", "tile")),
            P("dom", None),
            P("dom"),
        ),
        out_specs=(P(("dom", "tile"), None), P(("dom", "tile"), None), P(), P()),
        check_vma=False,
    )
```

```python
import functools

import jax
import jax.numpy as jnp
from jax import lax
from jax.experimental import pallas as pl
from jax.experimental.pallas import tpu as pltpu
from jax.sharding import PartitionSpec as P

BF = jnp.bfloat16
F32 = jnp.float32
MESH = pl.DeviceIdType.MESH
VMEM = pl.BlockSpec(memory_space=pltpu.VMEM)
SMEM = pl.BlockSpec(memory_space=pltpu.SMEM)
ANY = pl.BlockSpec(memory_space=pl.ANY)
LIMIT = 20 * 1024 * 1024
NT = (((1,), (1,)), ((), ()))
TN = (((0,), (0,)), ((), ()))


def places(domains):
    me = lax.axis_index("dom")
    t = lax.axis_index("tile")
    core = t + 1 - 2 * lax.rem(t, 2)
    across = lax.rem(t + 2, 4)
    diagonal = lax.rem(core + 2, 4)

    def slots(who):
        first = lax.rem(who + 4 * domains - me, 4)
        return lambda i: first + 4 * i

    return me, t, core, across, diagonal, slots


def remote(src, dst, send, recv, **device):
    return pltpu.make_async_remote_copy(
        src_ref=src,
        dst_ref=dst,
        send_sem=send,
        recv_sem=recv,
        device_id=device,
        device_id_type=MESH,
    )


def greet(me, peers, others, count, own):
    barrier = pltpu.get_barrier_semaphore()
    for peer in peers:
        pl.semaphore_signal(barrier, inc=1, device_id={"tile": peer}, device_id_type=MESH)
    for i in range(count):
        there = others(i)

        @pl.when(there != me)
        def _():
            pl.semaphore_signal(barrier, inc=1, device_id={"dom": there}, device_id_type=MESH)

    pl.semaphore_wait(barrier, len(peers) + count - own)


def met(me, mine, domains):
    return jnp.where(lax.rem(mine(0) + 4 * domains - me, 4) == 0, 1, 0)


def each(count, body):
    if count <= 4:
        for i in range(count):
            body(i)
    else:

        def step(i, carry):
            body(i)
            return carry

        lax.fori_loop(0, count, step, 0)


def dom_send(count, me, own_slots, pairs):
    def body(i):
        there = own_slots(i)
        for staged, landing, send, recv in pairs:

            @pl.when(there != me)
            def _():
                remote(staged.at[i], landing.at[me], send.at[i], recv.at[me], dom=there).start()

            @pl.when(there == me)
            def _():
                landing[me] = staged[i]

    each(count, body)


def dom_gather(count, me, t, core, across, diagonal, slots, pairs, forward):
    mine, theirs = slots(t), slots(across)

    def first(i):
        there = mine(i)
        for (staged, landing, send, recv), (fcore, facross) in zip(pairs, forward):

            @pl.when(there != me)
            def _():
                copy = remote(staged.at[i], landing.at[there], send.at[i], recv.at[there], dom=there)
                copy.wait_send()
                copy.wait_recv()

            spot = landing.at[there]
            remote(spot, spot, facross.at[there], recv.at[there], tile=across).start()
            remote(spot, spot, fcore.at[there], recv.at[there], tile=core).start()

    each(count, first)

    def second(i):
        there = theirs(i)
        for (staged, landing, send, recv), (fcore, facross) in zip(pairs, forward):
            spot = landing.at[there]
            remote(spot, spot, facross.at[there], recv.at[there], tile=across).wait_recv()
            remote(spot, spot, fcore.at[there], recv.at[there], tile=core).start()

    each(count, second)

    def third(i):
        for (staged, landing, send, recv), (fcore, facross) in zip(pairs, forward):
            for who in (core, diagonal):
                there = slots(who)(i)
                spot = landing.at[there]
                remote(spot, spot, fcore.at[there], recv.at[there], tile=core).wait_recv()
            for there, sem, peer in (
                (mine(i), facross, across),
                (mine(i), fcore, core),
                (theirs(i), fcore, core),
            ):
                spot = landing.at[there]
                remote(spot, spot, sem.at[there], recv.at[there], tile=peer).wait_send()

    each(count, third)


def tile_gather_start(src, out, t, core, across, send, recv):
    remote(src, out.at[t], send.at[0], recv.at[t], tile=across).start()
    remote(src, out.at[t], send.at[1], recv.at[t], tile=core).start()


def tile_gather_middle(out, core, across, send, recv):
    spot = out.at[across]
    remote(spot, spot, send.at[0], recv.at[across], tile=across).wait_recv()
    remote(spot, spot, send.at[2], recv.at[across], tile=core).start()


def tile_gather_end(src, out, core, across, diagonal, send, recv):
    for who in (core, diagonal):
        remote(out.at[who], out.at[who], send.at[1], recv.at[who], tile=core).wait_recv()
    tile_gather_sent(src, out, core, across, send, recv)


def tile_gather_sent(src, out, core, across, send, recv):
    remote(src, out.at[core], send.at[0], recv.at[core], tile=across).wait_send()
    remote(src, out.at[core], send.at[1], recv.at[core], tile=core).wait_send()
    remote(out.at[across], out.at[across], send.at[2], recv.at[core], tile=core).wait_send()


def collect_kernel(
    domains,
    feat,
    halo_ids,
    hub_ids,
    local,
    halo,
    hub,
    staged_halo,
    staged_hub,
    halo_acc,
    hub_acc,
    tile_send,
    tile_recv,
    halo_send,
    hub_send,
    halo_recv,
    hub_recv,
    halo_core,
    halo_across,
    hub_core,
    hub_across,
):
    count = domains // 4
    me, t, core, across, diagonal, slots = places(domains)
    mine = slots(t)
    quarter = feat.shape[0]
    greet(me, (core, across, diagonal), mine, count, met(me, mine, domains))
    tile_gather_start(feat, local, t, core, across, tile_send, tile_recv)
    local[t] = feat[...]

    def add(part, source, first):
        values = source[...]

        def term(ids):
            spot = lax.broadcasted_iota(jnp.int32, (quarter, ids.shape[1]), 0) + part * quarter
            chosen = (spot == ids).astype(F32).astype(BF)
            return lax.dot_general(chosen, values, TN, preferred_element_type=F32)

        def body(i):
            found = term(halo_ids[mine(i)])
            halo_acc[i] = found if first else halo_acc[i] + found

        each(count, body)
        found = term(hub_ids[...])
        hub_acc[...] = found if first else hub_acc[...] + found

    add(t, feat, True)
    remote(feat, local.at[core], tile_send.at[1], tile_recv.at[core], tile=core).wait_recv()
    add(core, local.at[core], False)
    tile_gather_middle(local, core, across, tile_send, tile_recv)
    add(across, local.at[across], False)
    remote(feat, local.at[diagonal], tile_send.at[2], tile_recv.at[diagonal], tile=core).wait_recv()
    add(diagonal, local.at[diagonal], False)
    own_hubs = hub_acc[...].astype(BF)

    def body(i):
        staged_hub[i] = own_hubs
        staged_halo[i] = halo_acc[i].astype(BF)

    each(count, body)
    pairs = ((staged_halo, halo, halo_send, halo_recv), (staged_hub, hub, hub_send, hub_recv))
    forward = ((halo_core, halo_across), (hub_core, hub_across))
    dom_send(count, me, mine, pairs)
    dom_gather(count, me, t, core, across, diagonal, slots, pairs, forward)
    tile_gather_sent(feat, local, core, across, tile_send, tile_recv)


def forward_kernel(tiles, dst, src, local, halo, hub, out, deg, source, acc, sems):
    nl, nh = local.shape[0], halo.shape[0]
    copies = [
        pltpu.make_async_copy(local, source.at[pl.ds(0, nl)], sems.at[0]),
        pltpu.make_async_copy(halo, source.at[pl.ds(nl, nh)], sems.at[1]),
        pltpu.make_async_copy(hub, source.at[pl.ds(nl + nh, hub.shape[0])], sems.at[2]),
    ]
    for copy in copies:
        copy.start()
    acc[...] = jnp.zeros_like(acc)
    deg[...] = jnp.zeros_like(deg)
    ones = jnp.ones((8, tiles.shape[2]), BF)
    for copy in copies:
        copy.wait()
    step = 4

    def body(k, carry):
        found = []
        for i in range(step):
            j = k * step + i
            e = tiles[j]
            found.append(
                (
                    dst[j],
                    jnp.dot(e, source[src[j]], preferred_element_type=F32),
                    lax.dot_general(ones, e, NT, preferred_element_type=F32),
                )
            )
        for d, product, weight in found:
            acc[d] += product
            deg[d] += weight
        return carry

    lax.fori_loop(0, tiles.shape[0] // step, body, 0)
    out[...] = acc[...].astype(BF)


def backward_kernel(tiles, dst, src, grad, active, local, halo, hub, active_out, acc, done):
    passing = pltpu.make_async_copy(active, active_out, done)
    passing.start()
    nl, nh = local.shape[0], halo.shape[0]
    acc[...] = jnp.zeros_like(acc)
    step = 4

    def body(k, carry):
        found = []
        for i in range(step):
            j = k * step + i
            found.append(
                (
                    src[j],
                    lax.dot_general(tiles[j], grad[dst[j]], TN, preferred_element_type=F32),
                )
            )
        for s, product in found:
            acc[s] += product
        return carry

    lax.fori_loop(0, tiles.shape[0] // step, body, 0)
    local[...] = acc[pl.ds(0, nl)].astype(BF)
    halo[...] = acc[pl.ds(nl, nh)].astype(BF)
    hub[...] = acc[pl.ds(nl + nh, hub.shape[0])].astype(BF)
    passing.wait()


def pair_send(partial, landing, send, recv, core, diagonal):
    remote(partial.at[diagonal], landing.at[1], send.at[1], recv.at[1], tile=core).start()
    remote(partial.at[core], landing.at[0], send.at[0], recv.at[0], tile=core).start()


def dense_kernel(
    domains,
    partial,
    deg,
    feat,
    grad_out,
    self_weight,
    neigh_weight,
    activated,
    grad_hidden,
    grad_all,
    terms,
    landing,
    other,
    passing,
    deg_in,
    mine_b,
    means,
    pair_sems,
    pair_recv,
    cross_sem,
    cross_recv,
    deg_send,
    deg_recv,
    tile_send,
    tile_recv,
):
    me, t, core, across, diagonal, slots = places(domains)
    chunks, rows = passing.shape[0], passing.shape[1]
    greet(me, (core, across, diagonal), None, 0, 0)
    pair_send(partial, landing, pair_sems, pair_recv, core, diagonal)
    peers = (core, across, diagonal)
    for i, peer in enumerate(peers):
        remote(deg.at[peer], deg_in.at[i], deg_send.at[i], deg_recv.at[i], tile=peer).start()
    first = remote(partial.at[across], landing.at[1], pair_sems.at[1], pair_recv.at[1], tile=core)
    first.wait_recv()
    crosses = []
    for c in range(chunks):
        span = pl.ds(c * rows, rows)
        passing[c] = (partial[across, span].astype(F32) + landing[1, span].astype(F32)).astype(BF)
        cross = remote(passing.at[c], other.at[c], cross_sem.at[c], cross_recv.at[c], tile=across)
        cross.start()
        crosses.append(cross)
    hidden_self = jnp.dot(feat[...], self_weight[...], preferred_element_type=F32)
    second = remote(partial.at[core], landing.at[0], pair_sems.at[0], pair_recv.at[0], tile=core)
    second.wait_recv()
    degree = deg[t]
    for i, peer in enumerate(peers):
        copy = remote(deg.at[peer], deg_in.at[i], deg_send.at[i], deg_recv.at[i], tile=peer)
        copy.wait_recv()
        degree = degree + deg_in[i]
    blocks, _, size = degree.shape
    columns = feat.shape[1]
    scale = 1.0 / jnp.maximum(degree, 1.0)
    pieces = []
    for b in range(blocks):
        turned = jnp.broadcast_to(scale[b, 0:1, :], (size, size)).T
        pieces.append(jnp.concatenate([turned] * (columns // size), axis=1))
    inverse_all = jnp.concatenate(pieces, axis=0)
    for c in range(chunks):
        span = pl.ds(c * rows, rows)
        inverse = inverse_all[c * rows : (c + 1) * rows]
        summed = partial[t, span].astype(F32) + landing[0, span].astype(F32)
        crosses[c].wait_recv()
        summed = summed + other[c].astype(F32)
        mean_rows = (summed * inverse).astype(BF)
        means[span] = mean_rows
        hidden = hidden_self[c * rows : (c + 1) * rows] + jnp.dot(
            mean_rows, neigh_weight[...], preferred_element_type=F32
        )
        sig = jax.nn.sigmoid(hidden)
        grads = (grad_out[span].astype(F32) * sig * (1.0 + hidden * (1.0 - sig))).astype(BF)
        back = lax.dot_general(grads, neigh_weight[...], NT, preferred_element_type=F32)
        mine_b[c] = (back * inverse).astype(BF)
        landed = grad_all.at[:, c]
        tile_gather_start(mine_b.at[c], landed, t, core, across, tile_send.at[c], tile_recv.at[c])
        grad_all[t, c] = mine_b[c]
        activated[span] = (hidden * sig).astype(BF)
        grad_hidden[span] = grads
    quarter = terms.shape[1]

    def term(values, place):
        found = lax.dot_general(values, grad_hidden[...], TN, preferred_element_type=F32)
        terms[place] = found[:quarter].astype(BF)
        terms[place + 1] = found[quarter:].astype(BF)

    term(feat[...], 0)
    for c in range(chunks):
        tile_gather_middle(grad_all.at[:, c], core, across, tile_send.at[c], tile_recv.at[c])
    term(means[...], 2)
    for c in range(chunks):
        tile_gather_end(
            mine_b.at[c], grad_all.at[:, c], core, across, diagonal, tile_send.at[c], tile_recv.at[c]
        )
    first.wait_send()
    second.wait_send()
    for cross in crosses:
        cross.wait_send()
    for i, peer in enumerate(peers):
        remote(deg.at[peer], deg_in.at[i], deg_send.at[i], deg_recv.at[i], tile=peer).wait_send()


def return_kernel(
    domains,
    inside,
    inv_root,
    local,
    halo,
    hub,
    halo_ids,
    hub_ids,
    grad_hidden,
    self_weight,
    terms,
    out,
    term_out,
    landing,
    other,
    passing,
    halo_in,
    hub_in,
    halo_pass,
    hub_pass,
    halo_other,
    hub_other,
    halo_total,
    hub_total,
    halo_back,
    hub_back,
    term_in,
    term_pass,
    term_other,
    term_cut,
    term_rs,
    term_sum,
    term_ag,
    term_mine,
    acc,
    pair_sems,
    pair_recv,
    cross_sem,
    cross_recv,
    halo_send,
    hub_send,
    halo_recv,
    hub_recv,
    halo_csend,
    hub_csend,
    halo_crecv,
    hub_crecv,
    halo_dsend,
    hub_dsend,
    halo_drecv,
    hub_drecv,
    halo_core,
    halo_across,
    hub_core,
    hub_across,
    term_psend,
    term_precv,
    term_csend,
    term_crecv,
    term_rsend,
    term_rrecv,
    term_asend,
    term_arecv,
    term_tsend,
    term_trecv,
):
    count = domains // 4
    me, t, core, across, diagonal, slots = places(domains)
    mine, theirs = slots(t), slots(across)
    quarter = out.shape[0]
    if inside:
        greet(me, (core, across, diagonal), lambda i: i, domains, 1)
    else:
        greet(me, (core, across, diagonal), mine, count, met(me, mine, domains))
    both = (
        (halo, halo_in, halo_send, halo_recv, halo_pass, halo_other, halo_csend, halo_crecv, halo_total),
        (hub, hub_in, hub_send, hub_recv, hub_pass, hub_other, hub_csend, hub_crecv, hub_total),
    )

    def start_for(who):
        spots = slots(who)

        def body(i):
            s = spots(i)
            for part, landed, send, recv, *_ in both:
                remote(part.at[s], landed.at[s], send.at[s], recv.at[s], tile=core).start()

        each(count, body)

    start_for(diagonal)
    start_for(core)
    if inside:
        pair_send(terms, term_in, term_psend, term_precv, core, diagonal)
    pair_send(local, landing, pair_sems, pair_recv, core, diagonal)

    def pass_on(i):
        s = theirs(i)
        for part, landed, send, recv, passed, crossed, csend, crecv, total in both:
            remote(part.at[s], landed.at[s], send.at[s], recv.at[s], tile=core).wait_recv()
            passed[i] = (part[s].astype(F32) + landed[s].astype(F32)).astype(BF)
            remote(passed.at[i], crossed.at[i], csend.at[i], crecv.at[i], tile=across).start()

    each(count, pass_on)
    if inside:
        term_first = remote(
            terms.at[across], term_in.at[1], term_psend.at[1], term_precv.at[1], tile=core
        )
        term_second = remote(
            terms.at[core], term_in.at[0], term_psend.at[0], term_precv.at[0], tile=core
        )
        term_cross = remote(
            term_pass, term_other, term_csend.at[0], term_crecv.at[0], tile=across
        )
        term_first.wait_recv()
        term_pass[...] = (terms[across].astype(F32) + term_in[1].astype(F32)).astype(BF)
        term_cross.start()
    first = remote(local.at[across], landing.at[1], pair_sems.at[1], pair_recv.at[1], tile=core)
    first.wait_recv()
    passing[...] = (local[across].astype(F32) + landing[1].astype(F32)).astype(BF)
    cross = remote(passing, other, cross_sem, cross_recv, tile=across)

    def own(i):
        s = mine(i)
        for part, landed, send, recv, passed, crossed, csend, crecv, total in both:
            remote(part.at[s], landed.at[s], send.at[s], recv.at[s], tile=core).wait_recv()
            remote(passed.at[i], crossed.at[i], csend.at[i], crecv.at[i], tile=across).wait_recv()
            total[i] = (part[s].astype(F32) + landed[s].astype(F32) + crossed[i].astype(F32)).astype(BF)

    each(count, own)
    pairs = (
        (halo_total, halo_back, halo_dsend, halo_drecv),
        (hub_total, hub_back, hub_dsend, hub_drecv),
    )
    forward = ((halo_core, halo_across), (hub_core, hub_across))
    dom_send(count, me, mine, pairs)
    cross.start()
    if inside:
        term_second.wait_recv()
        term_cross.wait_recv()
        cut = terms[t].astype(F32) + term_in[0].astype(F32) + term_other[...].astype(F32)
        term_cut[...] = cut.reshape(term_cut.shape)

        def to_all(source, landed, send, recv, start):
            for p in range(domains):

                @pl.when(p != me)
                def _():
                    if start:
                        remote(source(p), landed.at[me], send.at[p], recv.at[me], dom=p).start()
                    else:
                        remote(source(p), landed.at[p], send.at[p], recv.at[p], dom=p).wait_recv()

        def all_sent(source, landed, send, recv):
            for p in range(domains):

                @pl.when(p != me)
                def _():
                    remote(source(p), landed.at[p], send.at[p], recv.at[p], dom=p).wait_send()

        scatter = (lambda p: term_cut.at[p], term_rs, term_rsend, term_rrecv)
        collect = (lambda p: term_sum, term_ag, term_asend, term_arecv)
        to_all(*scatter, True)
        term_rs[me] = term_cut[me]
    acc[...] = lax.dot_general(grad_hidden[...], self_weight[...], NT, preferred_element_type=F32)
    second = remote(local.at[core], landing.at[0], pair_sems.at[0], pair_recv.at[0], tile=core)
    second.wait_recv()
    acc[...] += local[t].astype(F32) + landing[0].astype(F32)
    if inside:
        to_all(*scatter, False)
        term_sum[...] = jnp.sum(term_rs[...], axis=0) * inv_root
        to_all(*collect, True)
        term_ag[me] = term_sum[...]
    dom_gather(count, me, t, core, across, diagonal, slots, pairs, forward)
    if inside:
        to_all(*collect, False)
        term_mine[...] = term_ag[...].reshape(term_mine.shape)
        tile_gather_start(term_mine, term_out, t, core, across, term_tsend, term_trecv)
        term_out[t] = term_mine[...]

    def pick(ids):
        spot = lax.broadcasted_iota(jnp.int32, (quarter, ids.shape[1]), 0) + t * quarter
        return (spot == ids).astype(F32).astype(BF)

    hub_pick = pick(hub_ids[...])

    def spread(p, carry):
        acc[...] += jnp.dot(pick(halo_ids[p]), halo_back[p], preferred_element_type=F32) + jnp.dot(
            hub_pick, hub_back[p], preferred_element_type=F32
        )
        return carry

    lax.fori_loop(0, domains, spread, 0)
    cross.wait_recv()
    out[...] = (acc[...] + other[...].astype(F32)).astype(BF)
    if inside:
        tile_gather_middle(term_out, core, across, term_tsend, term_trecv)
        tile_gather_end(term_mine, term_out, core, across, diagonal, term_tsend, term_trecv)
        term_first.wait_send()
        term_second.wait_send()
        term_cross.wait_send()
        all_sent(*scatter)
        all_sent(*collect)
    else:
        term_out[...] = terms[...].astype(F32)
    first.wait_send()
    second.wait_send()
    cross.wait_send()

    def finish(i):
        for part, landed, send, recv, passed, crossed, csend, crecv, total in both:
            for who in (core, diagonal):
                s = slots(who)(i)
                remote(part.at[s], landed.at[s], send.at[s], recv.at[s], tile=core).wait_send()
            remote(passed.at[i], crossed.at[i], csend.at[i], crecv.at[i], tile=across).wait_send()

    each(count, finish)


def on_device(
    features,
    grad_out,
    self_weight,
    neigh_weight,
    edge_tiles,
    tile_dst,
    tile_src,
    halo_send,
    hub_ids,
):
    domains = lax.axis_size("dom")
    groups = lax.axis_size("tile")
    quarter, columns = features.shape
    size = edge_tiles.shape[1]
    vertices = quarter * groups
    halo_total = halo_send.shape[1]
    per_peer = halo_total // domains
    hub_own = hub_ids.shape[0]
    hubs = hub_own * domains
    count = domains // groups
    outs = grad_out.shape[1]
    nl, nh, nb = vertices // size, halo_total // size, hubs // size
    halo_ids = halo_send.reshape(domains, 1, per_peer)
    hub_row = hub_ids.reshape(1, hub_own)
    sem = lambda n: pltpu.SemaphoreType.DMA((n,))
    shape = jax.ShapeDtypeStruct

    def cost(mib):
        return pl.CostEstimate(flops=mib << 26, bytes_accessed=mib << 20, transcendentals=0)


    def params(number):
        return pltpu.CompilerParams(
            collective_id=number, has_side_effects=True, vmem_limit_bytes=LIMIT
        )

    local, halo, hub = pl.pallas_call(
        functools.partial(collect_kernel, domains),
        out_shape=(
            shape((groups, quarter, columns), BF),
            shape((domains, per_peer, columns), BF),
            shape((domains, hub_own, columns), BF),
        ),
        in_specs=[VMEM] * 3,
        out_specs=(VMEM,) * 3,
        scratch_shapes=[
            pltpu.VMEM((count, per_peer, columns), BF),
            pltpu.VMEM((count, hub_own, columns), BF),
            pltpu.VMEM((count, per_peer, columns), F32),
            pltpu.VMEM((hub_own, columns), F32),
            sem(3),
            sem(4),
            sem(count),
            sem(count),
        ]
        + [sem(domains)] * 6,
        compiler_params=params(0),
        cost_estimate=cost(30),
        name="collect",
    )(features, halo_ids, hub_row)

    partial, degree = pl.pallas_call(
        forward_kernel,
        out_shape=(shape((nl, size, columns), BF), shape((nl, 8, size), F32)),
        in_specs=[VMEM, SMEM, SMEM, ANY, ANY, ANY],
        out_specs=(VMEM, VMEM),
        scratch_shapes=[
            pltpu.VMEM((nl + nh + nb, size, columns), BF),
            pltpu.VMEM((nl, size, columns), F32),
            sem(3),
        ],
        compiler_params=pltpu.CompilerParams(vmem_limit_bytes=LIMIT),
        cost_estimate=cost(12),
        name="aggregate",
    )(
        edge_tiles,
        tile_dst,
        tile_src,
        local.reshape(nl, size, columns),
        halo.reshape(nh, size, columns),
        hub.reshape(nb, size, columns),
    )

    chunks = 2
    block = pltpu.VMEM((quarter, columns), BF)
    part = pltpu.VMEM((chunks, quarter // chunks, columns), BF)
    term_rows = 2 * columns // groups
    activated, grad_hidden, grad_all, terms = pl.pallas_call(
        functools.partial(dense_kernel, domains),
        out_shape=(
            shape((quarter, outs), BF),
            shape((quarter, outs), BF),
            shape((groups, chunks, quarter // chunks, columns), BF),
            shape((groups, term_rows, outs), BF),
        ),
        in_specs=[VMEM] * 6,
        out_specs=(VMEM,) * 4,
        scratch_shapes=[
            pltpu.VMEM((2, quarter, columns), BF),
            part,
            part,
            pltpu.VMEM((3, nl // groups, 8, size), F32),
            part,
            block,
            sem(2),
            sem(2),
            sem(chunks),
            sem(chunks),
            sem(3),
            sem(3),
            pltpu.SemaphoreType.DMA((chunks, 3)),
            pltpu.SemaphoreType.DMA((chunks, 4)),
        ],
        compiler_params=params(1),
        cost_estimate=cost(30),
        name="dense",
    )(
        partial.reshape(groups, quarter, columns),
        degree.reshape(groups, nl // groups, 8, size),
        features,
        grad_out,
        self_weight,
        neigh_weight,
    )

    inv_root = 1.0 / (vertices * domains) ** 0.5
    inside = term_rows % (8 * domains) == 0
    piece = pltpu.VMEM((domains, max(term_rows // domains, 8), outs), F32)

    back_local, back_halo, back_hub, activated = pl.pallas_call(
        backward_kernel,
        out_shape=(
            shape((nl, size, columns), BF),
            shape((nh, size, columns), BF),
            shape((nb, size, columns), BF),
            shape((quarter, outs), BF),
        ),
        in_specs=[VMEM, SMEM, SMEM, VMEM, ANY],
        out_specs=(VMEM,) * 3 + (ANY,),
        scratch_shapes=[
            pltpu.VMEM((nl + nh + nb, size, columns), F32),
            pltpu.SemaphoreType.DMA,
        ],
        cost_estimate=cost(12),
        compiler_params=pltpu.CompilerParams(vmem_limit_bytes=LIMIT),
        name="backward",
    )(edge_tiles, tile_dst, tile_src, grad_all.reshape(nl, size, columns), activated)

    term_shape = (term_rows, outs)
    grad_features, total = pl.pallas_call(
        functools.partial(return_kernel, domains, inside, inv_root),
        out_shape=(shape((quarter, columns), BF), shape((groups,) + term_shape, F32)),
        in_specs=[VMEM] * 8,
        out_specs=(VMEM, VMEM),
        scratch_shapes=[
            pltpu.VMEM((2, quarter, columns), BF),
            block,
            block,
            pltpu.VMEM((domains, per_peer, columns), BF),
            pltpu.VMEM((domains, hub_own, columns), BF),
            pltpu.VMEM((count, per_peer, columns), BF),
            pltpu.VMEM((count, hub_own, columns), BF),
            pltpu.VMEM((count, per_peer, columns), BF),
            pltpu.VMEM((count, hub_own, columns), BF),
            pltpu.VMEM((count, per_peer, columns), BF),
            pltpu.VMEM((count, hub_own, columns), BF),
            pltpu.VMEM((domains, per_peer, columns), BF),
            pltpu.VMEM((domains, hub_own, columns), BF),
            pltpu.VMEM((2,) + term_shape, BF),
            pltpu.VMEM(term_shape, BF),
            pltpu.VMEM(term_shape, BF),
            piece,
            piece,
            pltpu.VMEM(piece.shape[1:], F32),
            piece,
            pltpu.VMEM(term_shape, F32),
            pltpu.VMEM((quarter, columns), F32),
            sem(2),
            sem(2),
            pltpu.SemaphoreType.DMA,
            pltpu.SemaphoreType.DMA,
        ]
        + [sem(domains)] * 4
        + [sem(count)] * 4
        + [sem(count)] * 2
        + [sem(domains)] * 2
        + [sem(domains)] * 4
        + [sem(2)] * 2
        + [sem(1)] * 2
        + [sem(domains)] * 4
        + [sem(3), sem(4)],
        compiler_params=params(2),
        cost_estimate=cost(30),
        name="give_back",
    )(
        back_local.reshape(groups, quarter, columns),
        back_halo.reshape(domains, per_peer, columns),
        back_hub.reshape(domains, hub_own, columns),
        halo_ids,
        hub_row,
        grad_hidden,
        self_weight,
        terms,
    )
    if not inside:
        total = lax.psum(total, ("dom", "tile")) * inv_root
    both = total.reshape(2, columns, outs)
    return activated, grad_features, both[0], both[1]


def solution(mesh):
    return jax.shard_map(
        on_device,
        mesh=mesh,
        in_specs=(
            P(("dom", "tile"), None),
            P(("dom", "tile"), None),
            P(),
            P(),
            P(("dom", "tile"), None, None),
            P(("dom", "tile")),
            P(("dom", "tile")),
            P("dom", None),
            P("dom"),
        ),
        out_specs=(P(("dom", "tile"), None), P(("dom", "tile"), None), P(), P()),
        check_vma=False,
    )
```

```python
import functools

import jax
import jax.numpy as jnp
from jax import lax
from jax.experimental import pallas as pl
from jax.experimental.pallas import tpu as pltpu
from jax.sharding import PartitionSpec as P

BF = jnp.bfloat16
F32 = jnp.float32
MESH = pl.DeviceIdType.MESH
VMEM = pl.BlockSpec(memory_space=pltpu.VMEM)
SMEM = pl.BlockSpec(memory_space=pltpu.SMEM)
ANY = pl.BlockSpec(memory_space=pl.ANY)
LIMIT = 20 * 1024 * 1024
NT = (((1,), (1,)), ((), ()))
TN = (((0,), (0,)), ((), ()))


def places(domains):
    me = lax.axis_index("dom")
    t = lax.axis_index("tile")
    core = t + 1 - 2 * lax.rem(t, 2)
    across = lax.rem(t + 2, 4)
    diagonal = lax.rem(core + 2, 4)

    def slots(who):
        first = lax.rem(who + 4 * domains - me, 4)
        return lambda i: first + 4 * i

    return me, t, core, across, diagonal, slots


def remote(src, dst, send, recv, **device):
    return pltpu.make_async_remote_copy(
        src_ref=src,
        dst_ref=dst,
        send_sem=send,
        recv_sem=recv,
        device_id=device,
        device_id_type=MESH,
    )


def greet(me, peers, others, count, own):
    barrier = pltpu.get_barrier_semaphore()
    for peer in peers:
        pl.semaphore_signal(barrier, inc=1, device_id={"tile": peer}, device_id_type=MESH)
    for i in range(count):
        there = others(i)

        @pl.when(there != me)
        def _():
            pl.semaphore_signal(barrier, inc=1, device_id={"dom": there}, device_id_type=MESH)

    pl.semaphore_wait(barrier, len(peers) + count - own)


def met(me, mine, domains):
    return jnp.where(lax.rem(mine(0) + 4 * domains - me, 4) == 0, 1, 0)


def each(count, body):
    if count <= 4:
        for i in range(count):
            body(i)
    else:

        def step(i, carry):
            body(i)
            return carry

        lax.fori_loop(0, count, step, 0)


def dom_send(count, me, own_slots, pairs, ready=None):
    def body(i):
        there = own_slots(i)
        if ready is not None:
            ready(i)
        for staged, landing, send, recv in pairs:

            @pl.when(there != me)
            def _():
                remote(staged.at[i], landing.at[me], send.at[i], recv.at[me], dom=there).start()

            @pl.when(there == me)
            def _():
                landing[me] = staged[i]

    each(count, body)


def dom_gather(count, me, t, core, across, diagonal, slots, pairs, forward, between=None):
    mine, theirs = slots(t), slots(across)

    def first(i):
        there = mine(i)
        for (staged, landing, send, recv), (fcore, facross) in zip(pairs, forward):

            @pl.when(there != me)
            def _():
                copy = remote(staged.at[i], landing.at[there], send.at[i], recv.at[there], dom=there)
                copy.wait_send()
                copy.wait_recv()

            spot = landing.at[there]
            remote(spot, spot, facross.at[there], recv.at[there], tile=across).start()
            remote(spot, spot, fcore.at[there], recv.at[there], tile=core).start()

    each(count, first)
    if between is not None:
        between()

    def second(i):
        there = theirs(i)
        for (staged, landing, send, recv), (fcore, facross) in zip(pairs, forward):
            spot = landing.at[there]
            remote(spot, spot, facross.at[there], recv.at[there], tile=across).wait_recv()
            remote(spot, spot, fcore.at[there], recv.at[there], tile=core).start()

    each(count, second)

    def third(i):
        for (staged, landing, send, recv), (fcore, facross) in zip(pairs, forward):
            for who in (core, diagonal):
                there = slots(who)(i)
                spot = landing.at[there]
                remote(spot, spot, fcore.at[there], recv.at[there], tile=core).wait_recv()
            for there, sem, peer in (
                (mine(i), facross, across),
                (mine(i), fcore, core),
                (theirs(i), fcore, core),
            ):
                spot = landing.at[there]
                remote(spot, spot, sem.at[there], recv.at[there], tile=peer).wait_send()

    each(count, third)


def tile_gather_start(src, out, t, core, across, send, recv):
    remote(src, out.at[t], send.at[0], recv.at[t], tile=across).start()
    remote(src, out.at[t], send.at[1], recv.at[t], tile=core).start()


def tile_gather_middle(out, core, across, send, recv):
    spot = out.at[across]
    remote(spot, spot, send.at[0], recv.at[across], tile=across).wait_recv()
    remote(spot, spot, send.at[2], recv.at[across], tile=core).start()


def tile_gather_end(src, out, core, across, diagonal, send, recv):
    for who in (core, diagonal):
        remote(out.at[who], out.at[who], send.at[1], recv.at[who], tile=core).wait_recv()
    tile_gather_sent(src, out, core, across, send, recv)


def tile_gather_sent(src, out, core, across, send, recv):
    remote(src, out.at[core], send.at[0], recv.at[core], tile=across).wait_send()
    remote(src, out.at[core], send.at[1], recv.at[core], tile=core).wait_send()
    remote(out.at[across], out.at[across], send.at[2], recv.at[core], tile=core).wait_send()


def collect_kernel(
    domains,
    feat,
    halo_ids,
    hub_ids,
    local,
    halo,
    hub,
    staged_halo,
    staged_hub,
    halo_acc,
    hub_acc,
    tile_send,
    tile_recv,
    halo_send,
    hub_send,
    halo_recv,
    hub_recv,
    halo_core,
    halo_across,
    hub_core,
    hub_across,
):
    count = domains // 4
    me, t, core, across, diagonal, slots = places(domains)
    mine = slots(t)
    quarter = feat.shape[0]
    greet(me, (core, across, diagonal), mine, count, met(me, mine, domains))
    tile_gather_start(feat, local, t, core, across, tile_send, tile_recv)
    local[t] = feat[...]

    def term(ids, part, values):
        spot = lax.broadcasted_iota(jnp.int32, (quarter, ids.shape[1]), 0) + part * quarter
        chosen = (spot == ids).astype(F32).astype(BF)
        return lax.dot_general(chosen, values, TN, preferred_element_type=F32)

    def add(part, source, first):
        values = source[...]

        def body(i):
            found = term(halo_ids[mine(i)], part, values)
            halo_acc[i] = found if first else halo_acc[i] + found

        each(count, body)
        found = term(hub_ids[...], part, values)
        hub_acc[...] = found if first else hub_acc[...] + found

    add(t, feat, True)
    remote(feat, local.at[core], tile_send.at[1], tile_recv.at[core], tile=core).wait_recv()
    add(core, local.at[core], False)
    tile_gather_middle(local, core, across, tile_send, tile_recv)
    add(across, local.at[across], False)
    remote(feat, local.at[diagonal], tile_send.at[2], tile_recv.at[diagonal], tile=core).wait_recv()
    last = local[diagonal]
    own_hubs = (hub_acc[...] + term(hub_ids[...], diagonal, last)).astype(BF)

    def ready(i):
        staged_hub[i] = own_hubs
        staged_halo[i] = (halo_acc[i] + term(halo_ids[mine(i)], diagonal, last)).astype(BF)

    pairs = ((staged_halo, halo, halo_send, halo_recv), (staged_hub, hub, hub_send, hub_recv))
    forward = ((halo_core, halo_across), (hub_core, hub_across))
    dom_send(count, me, mine, pairs, ready)
    dom_gather(count, me, t, core, across, diagonal, slots, pairs, forward)
    tile_gather_sent(feat, local, core, across, tile_send, tile_recv)


def forward_kernel(tiles, dst, src, local, halo, hub, out, deg, source, acc, sems):
    nl, nh = local.shape[0], halo.shape[0]
    copies = [
        pltpu.make_async_copy(local, source.at[pl.ds(0, nl)], sems.at[0]),
        pltpu.make_async_copy(halo, source.at[pl.ds(nl, nh)], sems.at[1]),
        pltpu.make_async_copy(hub, source.at[pl.ds(nl + nh, hub.shape[0])], sems.at[2]),
    ]
    for copy in copies:
        copy.start()
    acc[...] = jnp.zeros_like(acc)
    deg[...] = jnp.zeros_like(deg)
    ones = jnp.ones((8, tiles.shape[2]), BF)
    for copy in copies:
        copy.wait()
    step = 8 if tiles.shape[0] % 8 == 0 else 1

    def body(k, carry):
        found = []
        for i in range(step):
            j = k * step + i
            e = tiles[j]
            found.append(
                (
                    dst[j],
                    jnp.dot(e, source[src[j]], preferred_element_type=F32),
                    lax.dot_general(ones, e, NT, preferred_element_type=F32),
                )
            )
        for d, product, weight in found:
            acc[d] += product
            deg[d] += weight
        return carry

    lax.fori_loop(0, tiles.shape[0] // step, body, 0)
    out[...] = acc[...].astype(BF)


def backward_kernel(tiles, dst, src, grad, active, local, halo, hub, active_out, acc, done):
    passing = pltpu.make_async_copy(active, active_out, done)
    passing.start()
    nl, nh = local.shape[0], halo.shape[0]
    acc[...] = jnp.zeros_like(acc)
    step = 8 if tiles.shape[0] % 8 == 0 else 1

    def body(k, carry):
        found = []
        for i in range(step):
            j = k * step + i
            found.append(
                (
                    src[j],
                    lax.dot_general(tiles[j], grad[dst[j]], TN, preferred_element_type=F32),
                )
            )
        for s, product in found:
            acc[s] += product
        return carry

    lax.fori_loop(0, tiles.shape[0] // step, body, 0)
    local[...] = acc[pl.ds(0, nl)].astype(BF)
    halo[...] = acc[pl.ds(nl, nh)].astype(BF)
    hub[...] = acc[pl.ds(nl + nh, hub.shape[0])].astype(BF)
    passing.wait()


def pair_send(partial, landing, send, recv, core, diagonal):
    remote(partial.at[diagonal], landing.at[1], send.at[1], recv.at[1], tile=core).start()
    remote(partial.at[core], landing.at[0], send.at[0], recv.at[0], tile=core).start()


def dense_kernel(
    domains,
    partial,
    deg,
    feat,
    grad_out,
    self_weight,
    neigh_weight,
    activated,
    grad_hidden,
    grad_all,
    terms,
    landing,
    other,
    passing,
    deg_in,
    mine_b,
    means,
    pair_sems,
    pair_recv,
    cross_sem,
    cross_recv,
    deg_send,
    deg_recv,
    tile_send,
    tile_recv,
):
    me, t, core, across, diagonal, slots = places(domains)
    chunks, rows = passing.shape[0], passing.shape[1]
    greet(me, (core, across, diagonal), None, 0, 0)
    pair_send(partial, landing, pair_sems, pair_recv, core, diagonal)
    peers = (core, across, diagonal)
    for i, peer in enumerate(peers):
        remote(deg.at[peer], deg_in.at[i], deg_send.at[i], deg_recv.at[i], tile=peer).start()
    first = remote(partial.at[across], landing.at[1], pair_sems.at[1], pair_recv.at[1], tile=core)
    first.wait_recv()
    crosses = []
    for c in range(chunks):
        span = pl.ds(c * rows, rows)
        passing[c] = (partial[across, span].astype(F32) + landing[1, span].astype(F32)).astype(BF)
        cross = remote(passing.at[c], other.at[c], cross_sem.at[c], cross_recv.at[c], tile=across)
        cross.start()
        crosses.append(cross)
    hidden_self = jnp.dot(feat[...], self_weight[...], preferred_element_type=F32)
    second = remote(partial.at[core], landing.at[0], pair_sems.at[0], pair_recv.at[0], tile=core)
    second.wait_recv()
    degree = deg[t]
    for i, peer in enumerate(peers):
        copy = remote(deg.at[peer], deg_in.at[i], deg_send.at[i], deg_recv.at[i], tile=peer)
        copy.wait_recv()
        degree = degree + deg_in[i]
    blocks, _, size = degree.shape
    columns = feat.shape[1]
    scale = 1.0 / jnp.maximum(degree, 1.0)
    pieces = []
    for b in range(blocks):
        turned = jnp.broadcast_to(scale[b, 0:1, :], (size, size)).T
        pieces.append(jnp.concatenate([turned] * (columns // size), axis=1))
    inverse_all = jnp.concatenate(pieces, axis=0)
    for c in range(chunks):
        span = pl.ds(c * rows, rows)
        inverse = inverse_all[c * rows : (c + 1) * rows]
        summed = partial[t, span].astype(F32) + landing[0, span].astype(F32)
        crosses[c].wait_recv()
        summed = summed + other[c].astype(F32)
        mean_rows = (summed * inverse).astype(BF)
        means[span] = mean_rows
        hidden = hidden_self[c * rows : (c + 1) * rows] + jnp.dot(
            mean_rows, neigh_weight[...], preferred_element_type=F32
        )
        sig = jax.nn.sigmoid(hidden)
        grads = (grad_out[span].astype(F32) * sig * (1.0 + hidden * (1.0 - sig))).astype(BF)
        back = lax.dot_general(grads, neigh_weight[...], NT, preferred_element_type=F32)
        mine_b[c] = (back * inverse).astype(BF)
        landed = grad_all.at[:, c]
        tile_gather_start(mine_b.at[c], landed, t, core, across, tile_send.at[c], tile_recv.at[c])
        grad_all[t, c] = mine_b[c]
        activated[span] = (hidden * sig).astype(BF)
        grad_hidden[span] = grads
    quarter = terms.shape[1]

    def term(values, place):
        found = lax.dot_general(values, grad_hidden[...], TN, preferred_element_type=F32)
        terms[place] = found[:quarter].astype(BF)
        terms[place + 1] = found[quarter:].astype(BF)

    term(feat[...], 0)
    for c in range(chunks):
        tile_gather_middle(grad_all.at[:, c], core, across, tile_send.at[c], tile_recv.at[c])
    term(means[...], 2)
    for c in range(chunks):
        tile_gather_end(
            mine_b.at[c], grad_all.at[:, c], core, across, diagonal, tile_send.at[c], tile_recv.at[c]
        )
    first.wait_send()
    second.wait_send()
    for cross in crosses:
        cross.wait_send()
    for i, peer in enumerate(peers):
        remote(deg.at[peer], deg_in.at[i], deg_send.at[i], deg_recv.at[i], tile=peer).wait_send()


def return_kernel(
    domains,
    inside,
    inv_root,
    local,
    halo,
    hub,
    halo_ids,
    hub_ids,
    grad_hidden,
    self_weight,
    terms,
    out,
    term_out,
    landing,
    other,
    passing,
    halo_in,
    hub_in,
    halo_pass,
    hub_pass,
    halo_other,
    hub_other,
    halo_total,
    hub_total,
    halo_back,
    hub_back,
    term_in,
    term_pass,
    term_other,
    term_cut,
    term_rs,
    term_sum,
    term_ag,
    term_mine,
    term_land,
    acc,
    pair_sems,
    pair_recv,
    cross_sem,
    cross_recv,
    halo_send,
    hub_send,
    halo_recv,
    hub_recv,
    halo_csend,
    hub_csend,
    halo_crecv,
    hub_crecv,
    halo_dsend,
    hub_dsend,
    halo_drecv,
    hub_drecv,
    halo_core,
    halo_across,
    hub_core,
    hub_across,
    term_psend,
    term_precv,
    term_csend,
    term_crecv,
    term_rsend,
    term_rrecv,
    term_asend,
    term_arecv,
    term_tsend,
    term_trecv,
):
    count = domains // 4
    me, t, core, across, diagonal, slots = places(domains)
    mine, theirs = slots(t), slots(across)
    quarter = out.shape[0]
    if inside:
        greet(me, (core, across, diagonal), lambda i: i, domains, 1)
    else:
        greet(me, (core, across, diagonal), mine, count, met(me, mine, domains))
    both = (
        (halo, halo_in, halo_send, halo_recv, halo_pass, halo_other, halo_csend, halo_crecv, halo_total),
        (hub, hub_in, hub_send, hub_recv, hub_pass, hub_other, hub_csend, hub_crecv, hub_total),
    )

    def start_for(who):
        spots = slots(who)

        def body(i):
            s = spots(i)
            for part, landed, send, recv, *_ in both:
                remote(part.at[s], landed.at[s], send.at[s], recv.at[s], tile=core).start()

        each(count, body)

    start_for(diagonal)
    start_for(core)
    if inside:
        pair_send(terms, term_in, term_psend, term_precv, core, diagonal)
    pair_send(local, landing, pair_sems, pair_recv, core, diagonal)

    def pass_on(i):
        s = theirs(i)
        for part, landed, send, recv, passed, crossed, csend, crecv, total in both:
            remote(part.at[s], landed.at[s], send.at[s], recv.at[s], tile=core).wait_recv()
            passed[i] = (part[s].astype(F32) + landed[s].astype(F32)).astype(BF)
            remote(passed.at[i], crossed.at[i], csend.at[i], crecv.at[i], tile=across).start()

    each(count, pass_on)
    if inside:
        term_first = remote(
            terms.at[across], term_in.at[1], term_psend.at[1], term_precv.at[1], tile=core
        )
        term_second = remote(
            terms.at[core], term_in.at[0], term_psend.at[0], term_precv.at[0], tile=core
        )
        term_cross = remote(
            term_pass, term_other, term_csend.at[0], term_crecv.at[0], tile=across
        )
        term_first.wait_recv()
        term_pass[...] = (terms[across].astype(F32) + term_in[1].astype(F32)).astype(BF)
        term_cross.start()
    first = remote(local.at[across], landing.at[1], pair_sems.at[1], pair_recv.at[1], tile=core)
    first.wait_recv()
    passing[...] = (local[across].astype(F32) + landing[1].astype(F32)).astype(BF)
    cross = remote(passing, other, cross_sem, cross_recv, tile=across)

    def own(i):
        s = mine(i)
        for part, landed, send, recv, passed, crossed, csend, crecv, total in both:
            remote(part.at[s], landed.at[s], send.at[s], recv.at[s], tile=core).wait_recv()
            remote(passed.at[i], crossed.at[i], csend.at[i], crecv.at[i], tile=across).wait_recv()
            total[i] = (part[s].astype(F32) + landed[s].astype(F32) + crossed[i].astype(F32)).astype(BF)

    each(count, own)
    pairs = (
        (halo_total, halo_back, halo_dsend, halo_drecv),
        (hub_total, hub_back, hub_dsend, hub_drecv),
    )
    forward = ((halo_core, halo_across), (hub_core, hub_across))
    dom_send(count, me, mine, pairs)
    cross.start()
    if inside:
        term_second.wait_recv()
        term_cross.wait_recv()
        cut = terms[t].astype(F32) + term_in[0].astype(F32) + term_other[...].astype(F32)
        term_cut[...] = cut.reshape(term_cut.shape).astype(BF)

        def to_all(source, landed, send, recv, start):
            for p in range(domains):

                @pl.when(p != me)
                def _():
                    if start:
                        remote(source(p), landed.at[me], send.at[p], recv.at[me], dom=p).start()
                    else:
                        remote(source(p), landed.at[p], send.at[p], recv.at[p], dom=p).wait_recv()

        def all_sent(source, landed, send, recv):
            for p in range(domains):

                @pl.when(p != me)
                def _():
                    remote(source(p), landed.at[p], send.at[p], recv.at[p], dom=p).wait_send()

        scatter = (lambda p: term_cut.at[p], term_rs, term_rsend, term_rrecv)
        collect = (lambda p: term_sum, term_ag, term_asend, term_arecv)
        to_all(*scatter, True)
        term_rs[me] = term_cut[me]
    acc[...] = lax.dot_general(grad_hidden[...], self_weight[...], NT, preferred_element_type=F32)
    second = remote(local.at[core], landing.at[0], pair_sems.at[0], pair_recv.at[0], tile=core)
    second.wait_recv()
    acc[...] += local[t].astype(F32) + landing[0].astype(F32)

    def between():
        to_all(*scatter, False)
        term_sum[...] = (jnp.sum(term_rs[...].astype(F32), axis=0) * inv_root).astype(BF)
        to_all(*collect, True)
        term_ag[me] = term_sum[...]

    dom_gather(
        count, me, t, core, across, diagonal, slots, pairs, forward, between if inside else None
    )
    if inside:
        to_all(*collect, False)
        term_mine[...] = term_ag[...].astype(F32).reshape(term_mine.shape).astype(BF)
        tile_gather_start(term_mine, term_land, t, core, across, term_tsend, term_trecv)
        term_land[t] = term_mine[...]

    def pick(ids):
        spot = lax.broadcasted_iota(jnp.int32, (quarter, ids.shape[1]), 0) + t * quarter
        return (spot == ids).astype(F32).astype(BF)

    hub_pick = pick(hub_ids[...])

    def spread(p, carry):
        acc[...] += jnp.dot(pick(halo_ids[p]), halo_back[p], preferred_element_type=F32) + jnp.dot(
            hub_pick, hub_back[p], preferred_element_type=F32
        )
        return carry

    lax.fori_loop(0, domains, spread, 0)
    cross.wait_recv()
    out[...] = (acc[...] + other[...].astype(F32)).astype(BF)
    if inside:
        tile_gather_middle(term_land, core, across, term_tsend, term_trecv)
        tile_gather_end(term_mine, term_land, core, across, diagonal, term_tsend, term_trecv)
        term_first.wait_send()
        term_second.wait_send()
        term_cross.wait_send()
        all_sent(*scatter)
        all_sent(*collect)
        term_out[...] = term_land[...].astype(F32)
    else:
        term_out[...] = terms[...].astype(F32)
    first.wait_send()
    second.wait_send()
    cross.wait_send()

    def finish(i):
        for part, landed, send, recv, passed, crossed, csend, crecv, total in both:
            for who in (core, diagonal):
                s = slots(who)(i)
                remote(part.at[s], landed.at[s], send.at[s], recv.at[s], tile=core).wait_send()
            remote(passed.at[i], crossed.at[i], csend.at[i], crecv.at[i], tile=across).wait_send()

    each(count, finish)


def on_device(
    features,
    grad_out,
    self_weight,
    neigh_weight,
    edge_tiles,
    tile_dst,
    tile_src,
    halo_send,
    hub_ids,
):
    domains = lax.axis_size("dom")
    groups = lax.axis_size("tile")
    quarter, columns = features.shape
    size = edge_tiles.shape[1]
    vertices = quarter * groups
    halo_total = halo_send.shape[1]
    per_peer = halo_total // domains
    hub_own = hub_ids.shape[0]
    hubs = hub_own * domains
    count = domains // groups
    outs = grad_out.shape[1]
    nl, nh, nb = vertices // size, halo_total // size, hubs // size
    halo_ids = halo_send.reshape(domains, 1, per_peer)
    hub_row = hub_ids.reshape(1, hub_own)
    sem = lambda n: pltpu.SemaphoreType.DMA((n,))
    shape = jax.ShapeDtypeStruct

    def cost(mib):
        return pl.CostEstimate(flops=mib << 26, bytes_accessed=mib << 20, transcendentals=0)


    def params(number):
        return pltpu.CompilerParams(
            collective_id=number, has_side_effects=True, vmem_limit_bytes=LIMIT
        )

    local, halo, hub = pl.pallas_call(
        functools.partial(collect_kernel, domains),
        out_shape=(
            shape((groups, quarter, columns), BF),
            shape((domains, per_peer, columns), BF),
            shape((domains, hub_own, columns), BF),
        ),
        in_specs=[VMEM] * 3,
        out_specs=(VMEM,) * 3,
        scratch_shapes=[
            pltpu.VMEM((count, per_peer, columns), BF),
            pltpu.VMEM((count, hub_own, columns), BF),
            pltpu.VMEM((count, per_peer, columns), F32),
            pltpu.VMEM((hub_own, columns), F32),
            sem(3),
            sem(4),
            sem(count),
            sem(count),
        ]
        + [sem(domains)] * 6,
        compiler_params=params(0),
        cost_estimate=cost(30),
        name="collect",
    )(features, halo_ids, hub_row)

    partial, degree = pl.pallas_call(
        forward_kernel,
        out_shape=(shape((nl, size, columns), BF), shape((nl, 8, size), F32)),
        in_specs=[VMEM, SMEM, SMEM, ANY, ANY, ANY],
        out_specs=(VMEM, VMEM),
        scratch_shapes=[
            pltpu.VMEM((nl + nh + nb, size, columns), BF),
            pltpu.VMEM((nl, size, columns), F32),
            sem(3),
        ],
        compiler_params=pltpu.CompilerParams(vmem_limit_bytes=LIMIT),
        cost_estimate=cost(12),
        name="aggregate",
    )(
        edge_tiles,
        tile_dst,
        tile_src,
        local.reshape(nl, size, columns),
        halo.reshape(nh, size, columns),
        hub.reshape(nb, size, columns),
    )

    chunks = 4
    block = pltpu.VMEM((quarter, columns), BF)
    part = pltpu.VMEM((chunks, quarter // chunks, columns), BF)
    term_rows = 2 * columns // groups
    activated, grad_hidden, grad_all, terms = pl.pallas_call(
        functools.partial(dense_kernel, domains),
        out_shape=(
            shape((quarter, outs), BF),
            shape((quarter, outs), BF),
            shape((groups, chunks, quarter // chunks, columns), BF),
            shape((groups, term_rows, outs), BF),
        ),
        in_specs=[VMEM] * 6,
        out_specs=(VMEM,) * 4,
        scratch_shapes=[
            pltpu.VMEM((2, quarter, columns), BF),
            part,
            part,
            pltpu.VMEM((3, nl // groups, 8, size), F32),
            part,
            block,
            sem(2),
            sem(2),
            sem(chunks),
            sem(chunks),
            sem(3),
            sem(3),
            pltpu.SemaphoreType.DMA((chunks, 3)),
            pltpu.SemaphoreType.DMA((chunks, 4)),
        ],
        compiler_params=params(1),
        cost_estimate=cost(30),
        name="dense",
    )(
        partial.reshape(groups, quarter, columns),
        degree.reshape(groups, nl // groups, 8, size),
        features,
        grad_out,
        self_weight,
        neigh_weight,
    )

    inv_root = 1.0 / (vertices * domains) ** 0.5
    inside = term_rows % (16 * domains) == 0
    piece = pltpu.VMEM((domains, max(term_rows // domains, 16), outs), BF)

    back_local, back_halo, back_hub, activated = pl.pallas_call(
        backward_kernel,
        out_shape=(
            shape((nl, size, columns), BF),
            shape((nh, size, columns), BF),
            shape((nb, size, columns), BF),
            shape((quarter, outs), BF),
        ),
        in_specs=[VMEM, SMEM, SMEM, VMEM, ANY],
        out_specs=(VMEM,) * 3 + (ANY,),
        scratch_shapes=[
            pltpu.VMEM((nl + nh + nb, size, columns), F32),
            pltpu.SemaphoreType.DMA,
        ],
        cost_estimate=cost(12),
        compiler_params=pltpu.CompilerParams(vmem_limit_bytes=LIMIT),
        name="backward",
    )(edge_tiles, tile_dst, tile_src, grad_all.reshape(nl, size, columns), activated)

    term_shape = (term_rows, outs)
    grad_features, total = pl.pallas_call(
        functools.partial(return_kernel, domains, inside, inv_root),
        out_shape=(shape((quarter, columns), BF), shape((groups,) + term_shape, F32)),
        in_specs=[VMEM] * 8,
        out_specs=(VMEM, VMEM),
        scratch_shapes=[
            pltpu.VMEM((2, quarter, columns), BF),
            block,
            block,
            pltpu.VMEM((domains, per_peer, columns), BF),
            pltpu.VMEM((domains, hub_own, columns), BF),
            pltpu.VMEM((count, per_peer, columns), BF),
            pltpu.VMEM((count, hub_own, columns), BF),
            pltpu.VMEM((count, per_peer, columns), BF),
            pltpu.VMEM((count, hub_own, columns), BF),
            pltpu.VMEM((count, per_peer, columns), BF),
            pltpu.VMEM((count, hub_own, columns), BF),
            pltpu.VMEM((domains, per_peer, columns), BF),
            pltpu.VMEM((domains, hub_own, columns), BF),
            pltpu.VMEM((2,) + term_shape, BF),
            pltpu.VMEM(term_shape, BF),
            pltpu.VMEM(term_shape, BF),
            piece,
            piece,
            pltpu.VMEM(piece.shape[1:], BF),
            piece,
            pltpu.VMEM(term_shape, BF),
            pltpu.VMEM((groups,) + term_shape, BF),
            pltpu.VMEM((quarter, columns), F32),
            sem(2),
            sem(2),
            pltpu.SemaphoreType.DMA,
            pltpu.SemaphoreType.DMA,
        ]
        + [sem(domains)] * 4
        + [sem(count)] * 4
        + [sem(count)] * 2
        + [sem(domains)] * 2
        + [sem(domains)] * 4
        + [sem(2)] * 2
        + [sem(1)] * 2
        + [sem(domains)] * 4
        + [sem(3), sem(4)],
        compiler_params=params(2),
        cost_estimate=cost(30),
        name="give_back",
    )(
        back_local.reshape(groups, quarter, columns),
        back_halo.reshape(domains, per_peer, columns),
        back_hub.reshape(domains, hub_own, columns),
        halo_ids,
        hub_row,
        grad_hidden,
        self_weight,
        terms,
    )
    if not inside:
        total = lax.psum(total, ("dom", "tile")) * inv_root
    both = total.reshape(2, columns, outs)
    return activated, grad_features, both[0], both[1]


def solution(mesh):
    return jax.shard_map(
        on_device,
        mesh=mesh,
        in_specs=(
            P(("dom", "tile"), None),
            P(("dom", "tile"), None),
            P(),
            P(),
            P(("dom", "tile"), None, None),
            P(("dom", "tile")),
            P(("dom", "tile")),
            P("dom", None),
            P("dom"),
        ),
        out_specs=(P(("dom", "tile"), None), P(("dom", "tile"), None), P(), P()),
        check_vma=False,
    )
```

```python
import functools

import jax
import jax.numpy as jnp
from jax import lax
from jax.experimental import pallas as pl
from jax.experimental.pallas import tpu as pltpu
from jax.sharding import PartitionSpec as P

BF = jnp.bfloat16
F32 = jnp.float32
MESH = pl.DeviceIdType.MESH
VMEM = pl.BlockSpec(memory_space=pltpu.VMEM)
SMEM = pl.BlockSpec(memory_space=pltpu.SMEM)
ANY = pl.BlockSpec(memory_space=pl.ANY)
LIMIT = 20 * 1024 * 1024
NT = (((1,), (1,)), ((), ()))
TN = (((0,), (0,)), ((), ()))


def places(domains):
    me = lax.axis_index("dom")
    t = lax.axis_index("tile")
    core = t + 1 - 2 * lax.rem(t, 2)
    across = lax.rem(t + 2, 4)
    diagonal = lax.rem(core + 2, 4)

    def slots(who):
        first = lax.rem(who + 4 * domains - me, 4)
        return lambda i: first + 4 * i

    return me, t, core, across, diagonal, slots


def remote(src, dst, send, recv, **device):
    return pltpu.make_async_remote_copy(
        src_ref=src,
        dst_ref=dst,
        send_sem=send,
        recv_sem=recv,
        device_id=device,
        device_id_type=MESH,
    )


def greet(me, peers, others, count, own):
    barrier = pltpu.get_barrier_semaphore()
    for peer in peers:
        pl.semaphore_signal(barrier, inc=1, device_id={"tile": peer}, device_id_type=MESH)
    for i in range(count):
        there = others(i)

        @pl.when(there != me)
        def _():
            pl.semaphore_signal(barrier, inc=1, device_id={"dom": there}, device_id_type=MESH)

    pl.semaphore_wait(barrier, len(peers) + count - own)


def met(me, mine, domains):
    return jnp.where(lax.rem(mine(0) + 4 * domains - me, 4) == 0, 1, 0)


def each(count, body):
    if count <= 4:
        for i in range(count):
            body(i)
    else:

        def step(i, carry):
            body(i)
            return carry

        lax.fori_loop(0, count, step, 0)


def dom_send(count, me, own_slots, pairs, ready=None):
    def body(i):
        there = own_slots(i)
        if ready is not None:
            ready(i)
        for staged, landing, send, recv in pairs:

            @pl.when(there != me)
            def _():
                remote(staged.at[i], landing.at[me], send.at[i], recv.at[me], dom=there).start()

            @pl.when(there == me)
            def _():
                landing[me] = staged[i]

    each(count, body)


def dom_gather(count, me, t, core, across, diagonal, slots, pairs, forward, between=None):
    mine, theirs = slots(t), slots(across)

    def first(i):
        there = mine(i)
        for (staged, landing, send, recv), (fcore, facross) in zip(pairs, forward):

            @pl.when(there != me)
            def _():
                copy = remote(staged.at[i], landing.at[there], send.at[i], recv.at[there], dom=there)
                copy.wait_send()
                copy.wait_recv()

            spot = landing.at[there]
            remote(spot, spot, facross.at[there], recv.at[there], tile=across).start()
            remote(spot, spot, fcore.at[there], recv.at[there], tile=core).start()

    each(count, first)
    if between is not None:
        between()

    def second(i):
        there = theirs(i)
        for (staged, landing, send, recv), (fcore, facross) in zip(pairs, forward):
            spot = landing.at[there]
            remote(spot, spot, facross.at[there], recv.at[there], tile=across).wait_recv()
            remote(spot, spot, fcore.at[there], recv.at[there], tile=core).start()

    each(count, second)

    def third(i):
        for (staged, landing, send, recv), (fcore, facross) in zip(pairs, forward):
            for who in (core, diagonal):
                there = slots(who)(i)
                spot = landing.at[there]
                remote(spot, spot, fcore.at[there], recv.at[there], tile=core).wait_recv()
            for there, sem, peer in (
                (mine(i), facross, across),
                (mine(i), fcore, core),
                (theirs(i), fcore, core),
            ):
                spot = landing.at[there]
                remote(spot, spot, sem.at[there], recv.at[there], tile=peer).wait_send()

    each(count, third)


def tile_gather_start(src, out, t, core, across, send, recv):
    remote(src, out.at[t], send.at[0], recv.at[t], tile=across).start()
    remote(src, out.at[t], send.at[1], recv.at[t], tile=core).start()


def tile_gather_middle(out, core, across, send, recv):
    spot = out.at[across]
    remote(spot, spot, send.at[0], recv.at[across], tile=across).wait_recv()
    remote(spot, spot, send.at[2], recv.at[across], tile=core).start()


def tile_gather_end(src, out, core, across, diagonal, send, recv):
    for who in (core, diagonal):
        remote(out.at[who], out.at[who], send.at[1], recv.at[who], tile=core).wait_recv()
    tile_gather_sent(src, out, core, across, send, recv)


def tile_gather_sent(src, out, core, across, send, recv):
    remote(src, out.at[core], send.at[0], recv.at[core], tile=across).wait_send()
    remote(src, out.at[core], send.at[1], recv.at[core], tile=core).wait_send()
    remote(out.at[across], out.at[across], send.at[2], recv.at[core], tile=core).wait_send()


def collect_kernel(
    domains,
    feat,
    halo_table,
    hub_table,
    local,
    halo,
    hub,
    halo_ids,
    hub_ids,
    id_sems,
    staged_halo,
    staged_hub,
    halo_acc,
    hub_acc,
    tile_send,
    tile_recv,
    halo_send,
    hub_send,
    halo_recv,
    hub_recv,
    halo_core,
    halo_across,
    hub_core,
    hub_across,
):
    count = domains // 4
    me, t, core, across, diagonal, slots = places(domains)
    mine = slots(t)
    quarter = feat.shape[0]
    halo_copy = pltpu.make_async_copy(halo_table, halo_ids, id_sems.at[0])
    hub_copy = pltpu.make_async_copy(hub_table, hub_ids, id_sems.at[1])
    halo_copy.start()
    hub_copy.start()
    greet(me, (core, across, diagonal), mine, count, met(me, mine, domains))
    tile_gather_start(feat, local, t, core, across, tile_send, tile_recv)
    local[t] = feat[...]

    def term(ids, part, values):
        spot = lax.broadcasted_iota(jnp.int32, (quarter, ids.shape[1]), 0) + part * quarter
        chosen = (spot == ids).astype(F32).astype(BF)
        return lax.dot_general(chosen, values, TN, preferred_element_type=F32)

    def add(part, source, first):
        values = source[...]

        def body(i):
            found = term(halo_ids[mine(i)], part, values)
            halo_acc[i] = found if first else halo_acc[i] + found

        each(count, body)
        found = term(hub_ids[...], part, values)
        hub_acc[...] = found if first else hub_acc[...] + found

    halo_copy.wait()
    hub_copy.wait()
    add(t, feat, True)
    remote(feat, local.at[core], tile_send.at[1], tile_recv.at[core], tile=core).wait_recv()
    add(core, local.at[core], False)
    tile_gather_middle(local, core, across, tile_send, tile_recv)
    add(across, local.at[across], False)
    remote(feat, local.at[diagonal], tile_send.at[2], tile_recv.at[diagonal], tile=core).wait_recv()
    last = local[diagonal]
    own_hubs = (hub_acc[...] + term(hub_ids[...], diagonal, last)).astype(BF)

    def ready(i):
        staged_hub[i] = own_hubs
        staged_halo[i] = (halo_acc[i] + term(halo_ids[mine(i)], diagonal, last)).astype(BF)

    pairs = ((staged_halo, halo, halo_send, halo_recv), (staged_hub, hub, hub_send, hub_recv))
    forward = ((halo_core, halo_across), (hub_core, hub_across))
    dom_send(count, me, mine, pairs, ready)
    dom_gather(count, me, t, core, across, diagonal, slots, pairs, forward)
    tile_gather_sent(feat, local, core, across, tile_send, tile_recv)


def forward_kernel(tiles, dst, src, local, halo, hub, out, deg, source, acc, sems):
    nl, nh = local.shape[0], halo.shape[0]
    copies = [
        pltpu.make_async_copy(local, source.at[pl.ds(0, nl)], sems.at[0]),
        pltpu.make_async_copy(halo, source.at[pl.ds(nl, nh)], sems.at[1]),
        pltpu.make_async_copy(hub, source.at[pl.ds(nl + nh, hub.shape[0])], sems.at[2]),
    ]
    for copy in copies:
        copy.start()
    acc[...] = jnp.zeros_like(acc)
    deg[...] = jnp.zeros_like(deg)
    ones = jnp.ones((8, tiles.shape[2]), BF)
    for copy in copies:
        copy.wait()
    step = 24 if tiles.shape[0] % 24 == 0 else 1

    def body(k, carry):
        found = []
        for i in range(step):
            j = k * step + i
            e = tiles[j]
            found.append(
                (
                    dst[j],
                    jnp.dot(e, source[src[j]], preferred_element_type=F32),
                    lax.dot_general(ones, e, NT, preferred_element_type=F32),
                )
            )
        for d, product, weight in found:
            acc[d] += product
            deg[d] += weight
        return carry

    lax.fori_loop(0, tiles.shape[0] // step, body, 0)
    out[...] = acc[...].astype(BF)


def backward_kernel(tiles, dst, src, grad, active, local, halo, hub, active_out, acc, done):
    passing = pltpu.make_async_copy(active, active_out, done)
    passing.start()
    nl, nh = local.shape[0], halo.shape[0]
    acc[...] = jnp.zeros_like(acc)
    step = 24 if tiles.shape[0] % 24 == 0 else 1

    def body(k, carry):
        found = []
        for i in range(step):
            j = k * step + i
            found.append(
                (
                    src[j],
                    lax.dot_general(tiles[j], grad[dst[j]], TN, preferred_element_type=F32),
                )
            )
        for s, product in found:
            acc[s] += product
        return carry

    lax.fori_loop(0, tiles.shape[0] // step, body, 0)
    local[...] = acc[pl.ds(0, nl)].astype(BF)
    halo[...] = acc[pl.ds(nl, nh)].astype(BF)
    hub[...] = acc[pl.ds(nl + nh, hub.shape[0])].astype(BF)
    passing.wait()


def pair_send(partial, landing, send, recv, core, diagonal):
    remote(partial.at[diagonal], landing.at[1], send.at[1], recv.at[1], tile=core).start()
    remote(partial.at[core], landing.at[0], send.at[0], recv.at[0], tile=core).start()


def dense_kernel(
    domains,
    partial,
    deg,
    feat,
    grad_out,
    self_weight,
    neigh_weight,
    activated,
    grad_hidden,
    grad_all,
    terms,
    landing,
    other,
    passing,
    deg_in,
    mine_b,
    means,
    pair_sems,
    pair_recv,
    cross_sem,
    cross_recv,
    deg_send,
    deg_recv,
    tile_send,
    tile_recv,
):
    me, t, core, across, diagonal, slots = places(domains)
    chunks, rows = passing.shape[0], passing.shape[1]
    greet(me, (core, across, diagonal), None, 0, 0)
    pair_send(partial, landing, pair_sems, pair_recv, core, diagonal)
    peers = (core, across, diagonal)
    for i, peer in enumerate(peers):
        remote(deg.at[peer], deg_in.at[i], deg_send.at[i], deg_recv.at[i], tile=peer).start()
    first = remote(partial.at[across], landing.at[1], pair_sems.at[1], pair_recv.at[1], tile=core)
    first.wait_recv()
    crosses = []
    for c in range(chunks):
        span = pl.ds(c * rows, rows)
        passing[c] = (partial[across, span].astype(F32) + landing[1, span].astype(F32)).astype(BF)
        cross = remote(passing.at[c], other.at[c], cross_sem.at[c], cross_recv.at[c], tile=across)
        cross.start()
        crosses.append(cross)
    hidden_self = jnp.dot(feat[...], self_weight[...], preferred_element_type=F32)
    second = remote(partial.at[core], landing.at[0], pair_sems.at[0], pair_recv.at[0], tile=core)
    second.wait_recv()
    degree = deg[t]
    for i, peer in enumerate(peers):
        copy = remote(deg.at[peer], deg_in.at[i], deg_send.at[i], deg_recv.at[i], tile=peer)
        copy.wait_recv()
        degree = degree + deg_in[i]
    blocks, _, size = degree.shape
    columns = feat.shape[1]
    scale = 1.0 / jnp.maximum(degree, 1.0)
    pieces = []
    for b in range(blocks):
        turned = jnp.broadcast_to(scale[b, 0:1, :], (size, size)).T
        pieces.append(jnp.concatenate([turned] * (columns // size), axis=1))
    inverse_all = jnp.concatenate(pieces, axis=0)
    for c in range(chunks):
        span = pl.ds(c * rows, rows)
        inverse = inverse_all[c * rows : (c + 1) * rows]
        summed = partial[t, span].astype(F32) + landing[0, span].astype(F32)
        crosses[c].wait_recv()
        summed = summed + other[c].astype(F32)
        mean_rows = (summed * inverse).astype(BF)
        means[span] = mean_rows
        hidden = hidden_self[c * rows : (c + 1) * rows] + jnp.dot(
            mean_rows, neigh_weight[...], preferred_element_type=F32
        )
        sig = jax.nn.sigmoid(hidden)
        grads = (grad_out[span].astype(F32) * sig * (1.0 + hidden * (1.0 - sig))).astype(BF)
        back = lax.dot_general(grads, neigh_weight[...], NT, preferred_element_type=F32)
        mine_b[c] = (back * inverse).astype(BF)
        landed = grad_all.at[:, c]
        tile_gather_start(mine_b.at[c], landed, t, core, across, tile_send.at[c], tile_recv.at[c])
        grad_all[t, c] = mine_b[c]
        activated[span] = (hidden * sig).astype(BF)
        grad_hidden[span] = grads
    quarter = terms.shape[1]

    def term(values, place):
        found = lax.dot_general(values, grad_hidden[...], TN, preferred_element_type=F32)
        terms[place] = found[:quarter].astype(BF)
        terms[place + 1] = found[quarter:].astype(BF)

    term(feat[...], 0)
    for c in range(chunks):
        tile_gather_middle(grad_all.at[:, c], core, across, tile_send.at[c], tile_recv.at[c])
    term(means[...], 2)
    for c in range(chunks):
        tile_gather_end(
            mine_b.at[c], grad_all.at[:, c], core, across, diagonal, tile_send.at[c], tile_recv.at[c]
        )
    first.wait_send()
    second.wait_send()
    for cross in crosses:
        cross.wait_send()
    for i, peer in enumerate(peers):
        remote(deg.at[peer], deg_in.at[i], deg_send.at[i], deg_recv.at[i], tile=peer).wait_send()


def return_kernel(
    domains,
    inside,
    inv_root,
    local,
    halo,
    hub,
    halo_ids,
    hub_ids,
    grad_hidden,
    self_weight,
    terms,
    out,
    term_out,
    landing,
    other,
    passing,
    halo_in,
    hub_in,
    halo_pass,
    hub_pass,
    halo_other,
    hub_other,
    halo_total,
    hub_total,
    halo_back,
    hub_back,
    term_in,
    term_pass,
    term_other,
    term_cut,
    term_rs,
    term_sum,
    term_ag,
    term_mine,
    term_land,
    acc,
    pair_sems,
    pair_recv,
    cross_sem,
    cross_recv,
    halo_send,
    hub_send,
    halo_recv,
    hub_recv,
    halo_csend,
    hub_csend,
    halo_crecv,
    hub_crecv,
    halo_dsend,
    hub_dsend,
    halo_drecv,
    hub_drecv,
    halo_core,
    halo_across,
    hub_core,
    hub_across,
    term_psend,
    term_precv,
    term_csend,
    term_crecv,
    term_rsend,
    term_rrecv,
    term_asend,
    term_arecv,
    term_tsend,
    term_trecv,
):
    count = domains // 4
    me, t, core, across, diagonal, slots = places(domains)
    mine, theirs = slots(t), slots(across)
    quarter = out.shape[0]
    if inside:
        greet(me, (core, across, diagonal), lambda i: i, domains, 1)
    else:
        greet(me, (core, across, diagonal), mine, count, met(me, mine, domains))
    both = (
        (halo, halo_in, halo_send, halo_recv, halo_pass, halo_other, halo_csend, halo_crecv, halo_total),
        (hub, hub_in, hub_send, hub_recv, hub_pass, hub_other, hub_csend, hub_crecv, hub_total),
    )

    def start_for(who):
        spots = slots(who)

        def body(i):
            s = spots(i)
            for part, landed, send, recv, *_ in both:
                remote(part.at[s], landed.at[s], send.at[s], recv.at[s], tile=core).start()

        each(count, body)

    start_for(diagonal)
    start_for(core)
    if inside:
        pair_send(terms, term_in, term_psend, term_precv, core, diagonal)
    pair_send(local, landing, pair_sems, pair_recv, core, diagonal)

    def pass_on(i):
        s = theirs(i)
        for part, landed, send, recv, passed, crossed, csend, crecv, total in both:
            remote(part.at[s], landed.at[s], send.at[s], recv.at[s], tile=core).wait_recv()
            passed[i] = (part[s].astype(F32) + landed[s].astype(F32)).astype(BF)
            remote(passed.at[i], crossed.at[i], csend.at[i], crecv.at[i], tile=across).start()

    each(count, pass_on)
    if inside:
        term_first = remote(
            terms.at[across], term_in.at[1], term_psend.at[1], term_precv.at[1], tile=core
        )
        term_second = remote(
            terms.at[core], term_in.at[0], term_psend.at[0], term_precv.at[0], tile=core
        )
        term_cross = remote(
            term_pass, term_other, term_csend.at[0], term_crecv.at[0], tile=across
        )
        term_first.wait_recv()
        term_pass[...] = (terms[across].astype(F32) + term_in[1].astype(F32)).astype(BF)
        term_cross.start()
    first = remote(local.at[across], landing.at[1], pair_sems.at[1], pair_recv.at[1], tile=core)
    first.wait_recv()
    passing[...] = (local[across].astype(F32) + landing[1].astype(F32)).astype(BF)
    cross = remote(passing, other, cross_sem, cross_recv, tile=across)

    def own(i):
        s = mine(i)
        for part, landed, send, recv, passed, crossed, csend, crecv, total in both:
            remote(part.at[s], landed.at[s], send.at[s], recv.at[s], tile=core).wait_recv()
            remote(passed.at[i], crossed.at[i], csend.at[i], crecv.at[i], tile=across).wait_recv()
            total[i] = (part[s].astype(F32) + landed[s].astype(F32) + crossed[i].astype(F32)).astype(BF)

    each(count, own)
    pairs = (
        (halo_total, halo_back, halo_dsend, halo_drecv),
        (hub_total, hub_back, hub_dsend, hub_drecv),
    )
    forward = ((halo_core, halo_across), (hub_core, hub_across))
    dom_send(count, me, mine, pairs)
    cross.start()
    if inside:
        term_second.wait_recv()
        term_cross.wait_recv()
        cut = terms[t].astype(F32) + term_in[0].astype(F32) + term_other[...].astype(F32)
        term_cut[...] = cut.reshape(term_cut.shape).astype(BF)

        def to_all(source, landed, send, recv, start):
            for p in range(domains):

                @pl.when(p != me)
                def _():
                    if start:
                        remote(source(p), landed.at[me], send.at[p], recv.at[me], dom=p).start()
                    else:
                        remote(source(p), landed.at[p], send.at[p], recv.at[p], dom=p).wait_recv()

        def all_sent(source, landed, send, recv):
            for p in range(domains):

                @pl.when(p != me)
                def _():
                    remote(source(p), landed.at[p], send.at[p], recv.at[p], dom=p).wait_send()

        scatter = (lambda p: term_cut.at[p], term_rs, term_rsend, term_rrecv)
        collect = (lambda p: term_sum, term_ag, term_asend, term_arecv)
        to_all(*scatter, True)
        term_rs[me] = term_cut[me]
    acc[...] = lax.dot_general(grad_hidden[...], self_weight[...], NT, preferred_element_type=F32)
    second = remote(local.at[core], landing.at[0], pair_sems.at[0], pair_recv.at[0], tile=core)
    second.wait_recv()
    acc[...] += local[t].astype(F32) + landing[0].astype(F32)

    def between():
        to_all(*scatter, False)
        term_sum[...] = (jnp.sum(term_rs[...].astype(F32), axis=0) * inv_root).astype(BF)
        to_all(*collect, True)
        term_ag[me] = term_sum[...]

    dom_gather(
        count, me, t, core, across, diagonal, slots, pairs, forward, between if inside else None
    )
    if inside:
        to_all(*collect, False)
        term_mine[...] = term_ag[...].astype(F32).reshape(term_mine.shape).astype(BF)
        tile_gather_start(term_mine, term_land, t, core, across, term_tsend, term_trecv)
        term_land[t] = term_mine[...]

    def pick(ids):
        spot = lax.broadcasted_iota(jnp.int32, (quarter, ids.shape[1]), 0) + t * quarter
        return (spot == ids).astype(F32).astype(BF)

    hub_pick = pick(hub_ids[...])

    def spread(p, carry):
        acc[...] += jnp.dot(pick(halo_ids[p]), halo_back[p], preferred_element_type=F32) + jnp.dot(
            hub_pick, hub_back[p], preferred_element_type=F32
        )
        return carry

    lax.fori_loop(0, domains, spread, 0)
    cross.wait_recv()
    out[...] = (acc[...] + other[...].astype(F32)).astype(BF)
    if inside:
        tile_gather_middle(term_land, core, across, term_tsend, term_trecv)
        tile_gather_end(term_mine, term_land, core, across, diagonal, term_tsend, term_trecv)
        term_first.wait_send()
        term_second.wait_send()
        term_cross.wait_send()
        all_sent(*scatter)
        all_sent(*collect)
        term_out[...] = term_land[...].astype(F32)
    else:
        term_out[...] = terms[...].astype(F32)
    first.wait_send()
    second.wait_send()
    cross.wait_send()

    def finish(i):
        for part, landed, send, recv, passed, crossed, csend, crecv, total in both:
            for who in (core, diagonal):
                s = slots(who)(i)
                remote(part.at[s], landed.at[s], send.at[s], recv.at[s], tile=core).wait_send()
            remote(passed.at[i], crossed.at[i], csend.at[i], crecv.at[i], tile=across).wait_send()

    each(count, finish)


def on_device(
    features,
    grad_out,
    self_weight,
    neigh_weight,
    edge_tiles,
    tile_dst,
    tile_src,
    halo_send,
    hub_ids,
):
    domains = lax.axis_size("dom")
    groups = lax.axis_size("tile")
    quarter, columns = features.shape
    size = edge_tiles.shape[1]
    vertices = quarter * groups
    halo_total = halo_send.shape[1]
    per_peer = halo_total // domains
    hub_own = hub_ids.shape[0]
    hubs = hub_own * domains
    count = domains // groups
    outs = grad_out.shape[1]
    nl, nh, nb = vertices // size, halo_total // size, hubs // size
    halo_ids = halo_send.reshape(domains, 1, per_peer)
    hub_row = hub_ids.reshape(1, hub_own)
    sem = lambda n: pltpu.SemaphoreType.DMA((n,))
    shape = jax.ShapeDtypeStruct

    def cost(mib):
        return pl.CostEstimate(flops=mib << 26, bytes_accessed=mib << 20, transcendentals=0)


    def params(number):
        return pltpu.CompilerParams(
            collective_id=number, has_side_effects=True, vmem_limit_bytes=LIMIT
        )

    local, halo, hub = pl.pallas_call(
        functools.partial(collect_kernel, domains),
        out_shape=(
            shape((groups, quarter, columns), BF),
            shape((domains, per_peer, columns), BF),
            shape((domains, hub_own, columns), BF),
        ),
        in_specs=[VMEM, ANY, ANY],
        out_specs=(VMEM,) * 3,
        scratch_shapes=[
            pltpu.VMEM((domains, 1, per_peer), jnp.int32),
            pltpu.VMEM((1, hub_own), jnp.int32),
            sem(2),
            pltpu.VMEM((count, per_peer, columns), BF),
            pltpu.VMEM((count, hub_own, columns), BF),
            pltpu.VMEM((count, per_peer, columns), F32),
            pltpu.VMEM((hub_own, columns), F32),
            sem(3),
            sem(4),
            sem(count),
            sem(count),
        ]
        + [sem(domains)] * 6,
        compiler_params=params(0),
        cost_estimate=cost(30),
        name="collect",
    )(features, halo_ids, hub_row)

    partial, degree = pl.pallas_call(
        forward_kernel,
        out_shape=(shape((nl, size, columns), BF), shape((nl, 8, size), F32)),
        in_specs=[VMEM, SMEM, SMEM, ANY, ANY, ANY],
        out_specs=(VMEM, VMEM),
        scratch_shapes=[
            pltpu.VMEM((nl + nh + nb, size, columns), BF),
            pltpu.VMEM((nl, size, columns), F32),
            sem(3),
        ],
        compiler_params=pltpu.CompilerParams(vmem_limit_bytes=LIMIT),
        cost_estimate=cost(12),
        name="aggregate",
    )(
        edge_tiles,
        tile_dst,
        tile_src,
        local.reshape(nl, size, columns),
        halo.reshape(nh, size, columns),
        hub.reshape(nb, size, columns),
    )

    chunks = 4
    block = pltpu.VMEM((quarter, columns), BF)
    part = pltpu.VMEM((chunks, quarter // chunks, columns), BF)
    term_rows = 2 * columns // groups
    activated, grad_hidden, grad_all, terms = pl.pallas_call(
        functools.partial(dense_kernel, domains),
        out_shape=(
            shape((quarter, outs), BF),
            shape((quarter, outs), BF),
            shape((groups, chunks, quarter // chunks, columns), BF),
            shape((groups, term_rows, outs), BF),
        ),
        in_specs=[VMEM] * 6,
        out_specs=(VMEM,) * 4,
        scratch_shapes=[
            pltpu.VMEM((2, quarter, columns), BF),
            part,
            part,
            pltpu.VMEM((3, nl // groups, 8, size), F32),
            part,
            block,
            sem(2),
            sem(2),
            sem(chunks),
            sem(chunks),
            sem(3),
            sem(3),
            pltpu.SemaphoreType.DMA((chunks, 3)),
            pltpu.SemaphoreType.DMA((chunks, 4)),
        ],
        compiler_params=params(1),
        cost_estimate=cost(30),
        name="dense",
    )(
        partial.reshape(groups, quarter, columns),
        degree.reshape(groups, nl // groups, 8, size),
        features,
        grad_out,
        self_weight,
        neigh_weight,
    )

    inv_root = 1.0 / (vertices * domains) ** 0.5
    inside = term_rows % (16 * domains) == 0
    piece = pltpu.VMEM((domains, max(term_rows // domains, 16), outs), BF)

    back_local, back_halo, back_hub, activated = pl.pallas_call(
        backward_kernel,
        out_shape=(
            shape((nl, size, columns), BF),
            shape((nh, size, columns), BF),
            shape((nb, size, columns), BF),
            shape((quarter, outs), BF),
        ),
        in_specs=[VMEM, SMEM, SMEM, VMEM, ANY],
        out_specs=(VMEM,) * 3 + (ANY,),
        scratch_shapes=[
            pltpu.VMEM((nl + nh + nb, size, columns), F32),
            pltpu.SemaphoreType.DMA,
        ],
        cost_estimate=cost(12),
        compiler_params=pltpu.CompilerParams(vmem_limit_bytes=LIMIT),
        name="backward",
    )(edge_tiles, tile_dst, tile_src, grad_all.reshape(nl, size, columns), activated)

    term_shape = (term_rows, outs)
    grad_features, total = pl.pallas_call(
        functools.partial(return_kernel, domains, inside, inv_root),
        out_shape=(shape((quarter, columns), BF), shape((groups,) + term_shape, F32)),
        in_specs=[VMEM] * 8,
        out_specs=(VMEM, VMEM),
        scratch_shapes=[
            pltpu.VMEM((2, quarter, columns), BF),
            block,
            block,
            pltpu.VMEM((domains, per_peer, columns), BF),
            pltpu.VMEM((domains, hub_own, columns), BF),
            pltpu.VMEM((count, per_peer, columns), BF),
            pltpu.VMEM((count, hub_own, columns), BF),
            pltpu.VMEM((count, per_peer, columns), BF),
            pltpu.VMEM((count, hub_own, columns), BF),
            pltpu.VMEM((count, per_peer, columns), BF),
            pltpu.VMEM((count, hub_own, columns), BF),
            pltpu.VMEM((domains, per_peer, columns), BF),
            pltpu.VMEM((domains, hub_own, columns), BF),
            pltpu.VMEM((2,) + term_shape, BF),
            pltpu.VMEM(term_shape, BF),
            pltpu.VMEM(term_shape, BF),
            piece,
            piece,
            pltpu.VMEM(piece.shape[1:], BF),
            piece,
            pltpu.VMEM(term_shape, BF),
            pltpu.VMEM((groups,) + term_shape, BF),
            pltpu.VMEM((quarter, columns), F32),
            sem(2),
            sem(2),
            pltpu.SemaphoreType.DMA,
            pltpu.SemaphoreType.DMA,
        ]
        + [sem(domains)] * 4
        + [sem(count)] * 4
        + [sem(count)] * 2
        + [sem(domains)] * 2
        + [sem(domains)] * 4
        + [sem(2)] * 2
        + [sem(1)] * 2
        + [sem(domains)] * 4
        + [sem(3), sem(4)],
        compiler_params=params(2),
        cost_estimate=cost(30),
        name="give_back",
    )(
        back_local.reshape(groups, quarter, columns),
        back_halo.reshape(domains, per_peer, columns),
        back_hub.reshape(domains, hub_own, columns),
        halo_ids,
        hub_row,
        grad_hidden,
        self_weight,
        terms,
    )
    if not inside:
        total = lax.psum(total, ("dom", "tile")) * inv_root
    both = total.reshape(2, columns, outs)
    return activated, grad_features, both[0], both[1]


def solution(mesh):
    return jax.shard_map(
        on_device,
        mesh=mesh,
        in_specs=(
            P(("dom", "tile"), None),
            P(("dom", "tile"), None),
            P(),
            P(),
            P(("dom", "tile"), None, None),
            P(("dom", "tile")),
            P(("dom", "tile")),
            P("dom", None),
            P("dom"),
        ),
        out_specs=(P(("dom", "tile"), None), P(("dom", "tile"), None), P(), P()),
        check_vma=False,
    )
```
